128 devices in a mesh: rows: 16 (over y, z), cols: 8 (over x, core).
Axes of the slice: x: 4, y: 4, z: 4, core: 2. Of those that a mesh axis runs over, the one named last changes fastest.
Arguments:
- series: float32 [300, 32768], P(None, ('rows', 'cols')), may hold values from -6 to 6
- point_order: int32 [32768], P('rows'), may hold values from 0 to 32767, as said below
- step_block: int32 [8], replicated, may hold values from 16 to 31, as said below
- panel: float32 [32768, 8192], P('rows', 'cols'), may hold values from -0.09375 to 0.09375
- diag_inverse: float32 [32768, 1024], P('rows'), may hold values from -0.09375 to 1.09375
Outputs:
- solved: float32 [8192, 300], P(('rows', 'cols'))
- residual: float32 [32768, 300], P(('rows', 'cols'))
The draws below stay inside these ranges and needn't reach their ends.
Inputs may be any that keep to these rules, and one draw needn't show every extreme that they name: Within each group of 2048 consecutive points, point_order is a permutation of the same group's indices. `step_block`: step k lies in block rows k * 2 + c to k * 2 + c + 1, with c = 16; the first step takes the first row of its range and the last step the last row of its range.
All inputs are finite; a program needn't handle non-finite values.
Results may differ from the reference program's by a relative error of at most 0.00014.
Values sent between devices are 32-bit elements; how exact they have to be, the bound alone decides.
A program may use at most 128 MiB of HBM per device.

```python
import jax
import jax.numpy as jnp
from jax import lax

BS = 1024
DATES = 300
STEPS = 8
BR_DEV = 2
NBLK = 32
POINTS = 32768
SOLVED = 8192


def draw_point_order(key, part):
    group_size = BR_DEV * BS
    groups = POINTS // group_size
    keys = jax.random.split(key, groups)
    orders = jax.vmap(lambda single: jax.random.permutation(single, group_size))(keys)
    offsets = jnp.arange(groups, dtype=jnp.int32)[:, None] * group_size
    return (orders.astype(jnp.int32) + offsets).reshape(-1)


def draw_step_block(key, part):
    second = jax.random.fold_in(key, 11)
    groups = NBLK // BR_DEV
    offset = groups - STEPS
    slots = jax.random.randint(second, (STEPS,), 0, BR_DEV)
    positions = jnp.arange(STEPS, dtype=jnp.int32)
    slots = jnp.where(positions == 0, 0, slots)
    slots = jnp.where(positions == STEPS - 1, BR_DEV - 1, slots)
    owners = positions + offset
    return (owners * BR_DEV + slots).astype(jnp.int32)


def draw_diag_inverse(key, part):
    total_rows = NBLK * BS
    noise = jnp.clip(jax.random.normal(key, (total_rows, BS), jnp.float32), -6.0, 6.0)
    identity = (jnp.arange(total_rows)[:, None] % BS == jnp.arange(BS)[None, :]).astype(jnp.float32)
    return identity + 0.5 * noise * BS ** (-0.5)


def block_levels(key, dims, cuts, least, top_value):
    def one(position, blocks):
        draws = jax.random.uniform(jax.random.fold_in(jax.random.fold_in(key, 6), position), (blocks,), jnp.float32, least / len(cuts), top_value / len(cuts))
        return jnp.repeat(jnp.exp(draws), dims[position] // blocks).reshape((-1,) + (1,) * (len(dims) - position - 1))

    gain = one(*cuts[0])
    for cut in cuts[1:]:
        gain = gain * one(*cut)
    return gain


def bell_draw(own_key, extent, width, bound, cuts=(), kind=jnp.bfloat16):
    factor_of = block_levels(own_key, extent, cuts, -0.22, 0.18) if cuts else 1.0
    values = jax.random.normal(own_key, extent, jnp.float32) * width * factor_of
    return jnp.minimum(jnp.maximum(values, -bound), bound).astype(kind)


def setup_inputs(seed: int = 0) -> dict:
    arg_keys = jax.random.split(jax.random.key(seed), 6)
    return {
        "series": bell_draw(arg_keys[0], (DATES, POINTS), 1.0, 6.0, ((1, 128),), jnp.float32),
        "point_order": draw_point_order(jax.random.fold_in(arg_keys[5], 71), 0),
        "step_block": draw_step_block(jax.random.fold_in(arg_keys[5], 71), 0),
        "panel": bell_draw(arg_keys[3], (POINTS, SOLVED), (4 * STEPS * BS // 9) ** -0.5, 0.09375, ((0, 16), (1, 8)), jnp.float32),
        "diag_inverse": draw_diag_inverse(jax.random.fold_in(arg_keys[5], 71), 0),
    }


def reference(series, point_order, step_block, panel, diag_inverse):
    right_side = jnp.take(series, point_order, axis=1).T
    highest = lax.Precision.HIGHEST
    pieces = []
    for section in range(STEPS):
        start = (step_block[section] * BS).astype(jnp.int32)
        partial_value = jnp.zeros((BS, DATES), jnp.float32)
        for earlier in range(section):
            factor_block = lax.dynamic_slice(panel, (start, jnp.int32(earlier * BS)), (BS, BS))
            partial_value = partial_value + jnp.dot(factor_block, pieces[earlier], precision=highest, preferred_element_type=jnp.float32)
        pivot = lax.dynamic_slice(right_side, (start, jnp.int32(0)), (BS, DATES)) - partial_value
        inverse = lax.dynamic_slice(diag_inverse, (start, jnp.int32(0)), (BS, BS))
        pieces.append(jnp.dot(inverse, pivot, precision=highest, preferred_element_type=jnp.float32))
    solved = jnp.concatenate(pieces, axis=0)
    residual = right_side - jnp.dot(panel, solved, precision=highest, preferred_element_type=jnp.float32)
    return solved, residual
```

```python
import jax
import jax.numpy as jnp
from jax import lax
from jax.experimental import pallas as pl
from jax.experimental.pallas import tpu as pltpu
from jax.sharding import PartitionSpec as P

MESH = pl.DeviceIdType.MESH
F32 = jnp.float32
BF16 = jnp.bfloat16
CHUNKS = 5
CD = 64
BS = 1024
COLS = 8
PIECE = 256
FIRST = 8


def split2(v):
    hi = v.astype(BF16)
    return hi, (v - hi.astype(F32)).astype(BF16)


def split3(v):
    hi = v.astype(BF16)
    rest = v - hi.astype(F32)
    mid = rest.astype(BF16)
    return hi, mid, (rest - mid.astype(F32)).astype(BF16)


def nt(a, b):
    return lax.dot_general(a, b, (((1,), (1,)), ((), ())), preferred_element_type=F32)


def nn(a, b):
    return lax.dot_general(a, b, (((1,), (0,)), ((), ())), preferred_element_type=F32)


def kernel(step_ref, idx_ref, ser_ref, panel_ref, diag_ref, res_ref, sol_ref,
           pf, df, phi, plo, mhi, mlo, dhi, dlo, oh, ohr, gbuf, xbuf, pbuf, obuf, zbuf, rbuf, sbuf,
           pl_sem, dl_sem, gs_sem, gr_sem, f_sem, x_sem, o_sem, p_sem, zs_sem, zr_sem, ss_sem, sr_sem):
    r = lax.axis_index("rows")
    c = lax.axis_index("cols")
    k = r - FIRST
    y, z = r // 4, r % 4
    root = FIRST + 1 + jnp.minimum(c, 6)
    dy = (y - root // 4 + 4) % 4
    dz = (z - root % 4 + 4) % 4
    late = r >= FIRST
    chain = jnp.logical_and(late, c < k)
    starts = jnp.logical_and(late, c == 7)
    uses_d = jnp.logical_or(chain, starts)
    final_col = (k + 15) % 8
    final = jnp.logical_and(late, c == final_col)
    produces = uses_d
    diag_src = jnp.logical_and(final, r < 15)
    diag_dst = jnp.logical_and(c < 7, r == root)
    out_row = jnp.minimum(r + 1, 15)
    prev_col = (c + 7) % 8
    next_col = (c + 1) % 8

    zp, zm = y * 4 + (z + 1) % 4, y * 4 + (z + 3) % 4
    yp, ym = ((y + 1) % 4) * 4 + z, ((y + 3) % 4) * 4 + z

    barrier = pltpu.get_barrier_semaphore()
    for other in (zp, zm, yp, ym):
        pl.semaphore_signal(barrier, inc=1, device_id=(other, c), device_id_type=MESH)
    for d in range(1, COLS):
        pl.semaphore_signal(barrier, inc=1, device_id=(r, (c + d) % COLS), device_id_type=MESH)

    @pl.when(diag_src)
    def _():
        pl.semaphore_signal(barrier, inc=1, device_id=(out_row, k), device_id_type=MESH)

    @pl.when(diag_dst)
    def _():
        pl.semaphore_signal(barrier, inc=1, device_id=(r - 1, prev_col), device_id_type=MESH)

    def load_d(j):
        return pltpu.make_async_copy(diag_ref.at[pl.ds(j * PIECE, PIECE)], df.at[pl.ds(j * PIECE, PIECE)], dl_sem.at[j])

    def load_p(j):
        return pltpu.make_async_copy(panel_ref.at[pl.ds(j * PIECE, PIECE)], pf.at[pl.ds(j * PIECE, PIECE)], pl_sem.at[j])

    @pl.when(uses_d)
    def _():
        for j in range(8):
            load_d(j).start()

    for j in range(8):
        load_p(j).start()

    pl.semaphore_wait(barrier, 11 + diag_src.astype(jnp.int32) + diag_dst.astype(jnp.int32))

    def g_copy(src, i):
        return pltpu.make_async_remote_copy(
            src_ref=ser_ref.at[i], dst_ref=gbuf.at[src, i], send_sem=gs_sem.at[i],
            recv_sem=gr_sem.at[src, i], device_id=(r, 7), device_id_type=MESH)

    def x_copy(e, i, row):
        return pltpu.make_async_remote_copy(
            src_ref=xbuf.at[i], dst_ref=xbuf.at[i], send_sem=f_sem.at[e, i],
            recv_sem=x_sem.at[i], device_id=(row, c), device_id_type=MESH)

    def out_copy(i):
        return pltpu.make_async_remote_copy(
            src_ref=obuf.at[i], dst_ref=xbuf.at[i], send_sem=o_sem.at[i],
            recv_sem=x_sem.at[i], device_id=(out_row, k), device_id_type=MESH)

    def part_copy(i):
        return pltpu.make_async_remote_copy(
            src_ref=obuf.at[i], dst_ref=pbuf.at[i], send_sem=o_sem.at[i],
            recv_sem=p_sem.at[i], device_id=(r, next_col), device_id_type=MESH)

    def z_copy(i, d):
        return pltpu.make_async_remote_copy(
            src_ref=zbuf.at[i, d], dst_ref=rbuf.at[c, i], send_sem=zs_sem.at[i, d],
            recv_sem=zr_sem.at[c, i], device_id=(r, d), device_id_type=MESH)

    def z_wait(src, i):
        pltpu.make_async_remote_copy(
            src_ref=zbuf.at[i, src], dst_ref=rbuf.at[src, i], send_sem=zs_sem.at[i, src],
            recv_sem=zr_sem.at[src, i], device_id=(r, src), device_id_type=MESH).wait_recv()

    solver_col = r // 2
    sol_src = c == solver_col

    def s_copy(i, d):
        lane = pl.multiple_of((r % 2) * 512 + (d // 2) * 128, 128)
        return pltpu.make_async_remote_copy(
            src_ref=xbuf.at[i, :, pl.ds(lane, 128)], dst_ref=sbuf.at[i], send_sem=ss_sem.at[i, d],
            recv_sem=sr_sem.at[i], device_id=(r, d), device_id_type=MESH)

    edges = (
        (jnp.logical_and(dy == 0, dz <= 1), zp),
        (jnp.logical_and(dy == 0, dz == 0), zm),
        (dy <= 1, yp),
        (dy == 0, ym),
    )

    def send_out(i):
        @pl.when(final)
        def _():
            out_copy(i).start()

        @pl.when(jnp.logical_not(final))
        def _():
            part_copy(i).start()

    @pl.when(jnp.logical_and(late, c < 7))
    def _():
        @pl.loop(0, CHUNKS)
        def _(i):
            g_copy(c, i).start()

    slot = step_ref[jnp.maximum(k, 0)] - 2 * r

    def pick(first, second):
        return jnp.where(jnp.full(first.shape, slot, jnp.int32) == 0, first, second)

    shift = r * (COLS * PIECE)

    @pl.when(uses_d)
    def _():
        @pl.loop(0, 8)
        def _(j):
            load_d(j).wait()

        @pl.loop(0, 8)
        def _(j):
            rows = pl.ds(pl.multiple_of(j * 128, 128), 128)
            hi, lo = split2(pick(df[rows, :], df[pl.ds(pl.multiple_of(BS + j * 128, 128), 128), :]))
            dhi[rows, :] = hi
            dlo[rows, :] = lo

    @pl.when(starts)
    def _():
        for q in range(4):
            want = pick(idx_ref[q:q + 1, :], idx_ref[4 + q:5 + q, :]) - shift

            @pl.loop(0, COLS)
            def _(s):
                pos = lax.broadcasted_iota(jnp.int32, (PIECE, PIECE), 0) + s * PIECE
                oh[pl.ds(pl.multiple_of(s * PIECE, PIECE), PIECE), q * PIECE:(q + 1) * PIECE] = (
                    jnp.where(pos == want, 1.0, 0.0).astype(BF16))

        @pl.loop(0, CHUNKS)
        def _(i):
            hi, lo = split2(ser_ref[i])
            acc = nn(jnp.concatenate([hi, lo], axis=0), oh[7 * PIECE:, :])
            for s in range(7):
                pltpu.make_async_remote_copy(
                    src_ref=ser_ref.at[i], dst_ref=gbuf.at[s, i], send_sem=gs_sem.at[i],
                    recv_sem=gr_sem.at[s, i], device_id=(r, s), device_id_type=MESH).wait_recv()
                hi, lo = split2(gbuf[s, i])
                acc = acc + nn(jnp.concatenate([hi, lo], axis=0), oh[s * PIECE:(s + 1) * PIECE, :])
            both = acc.astype(BF16)
            out = nt(both, dhi[...])
            obuf[i] = out[:CD] + out[CD:] + nt(both[:CD], dlo[...])
            send_out(i)

    @pl.loop(0, 8)
    def _(j):
        load_p(j).wait()
        rows = pl.ds(pl.multiple_of(j * PIECE, PIECE), PIECE)
        hi, lo = split2(pf[rows, :])
        phi[rows, :] = hi
        plo[rows, :] = lo

    @pl.when(chain)
    def _():
        @pl.loop(0, 8)
        def _(j):
            rows = pl.ds(pl.multiple_of(j * 128, 128), 128)
            other = pl.ds(pl.multiple_of(BS + j * 128, 128), 128)
            hi, lo = split2(pick(pf[rows, :], pf[other, :]))
            oh[rows, :] = hi
            oh[other, :] = lo

        @pl.loop(0, 4)
        def _(j):
            rows = pl.ds(pl.multiple_of(j * PIECE, PIECE), PIECE)
            th = dhi[rows, :]
            ph = oh[:BS, :]
            m = nn(th, ph) + nn(dlo[rows, :], ph) + nn(th, oh[BS:, :])
            hi, lo = split2(m)
            mhi[rows, :] = hi
            mlo[rows, :] = lo

    @pl.loop(0, COLS)
    def _(d):
        want = idx_ref[pl.ds(d, 1), :] - shift
        pos = lax.broadcasted_iota(jnp.int32, (PIECE, PIECE), 0) + c * PIECE
        ohr[d] = jnp.where(pos == want, 1.0, 0.0).astype(BF16)

    def residual(i):
        hi, lo = split2(xbuf[i])
        both = jnp.concatenate([hi, lo], axis=0)
        three = jnp.concatenate(split3(ser_ref[i]), axis=0)

        @pl.loop(0, COLS)
        def _(d):
            rows = pl.ds(pl.multiple_of(d * PIECE, PIECE), PIECE)
            a = nt(both, phi[rows, :])
            a = a[:CD] + a[CD:] + nt(hi, plo[rows, :])
            b = nn(three, ohr[d])
            b = b[:CD] + (b[CD:2 * CD] + b[2 * CD:])

            @pl.when(d == c)
            def _():
                rbuf[c, i] = b - a

            @pl.when(d != c)
            def _():
                zbuf[i, d] = b - a
                z_copy(i, d).start()

    @pl.loop(0, CHUNKS)
    def _(i):
        x_copy(0, i, zp).wait_recv()
        for e, (cond, row) in enumerate(edges):
            @pl.when(cond)
            def _():
                x_copy(e, i, row).start()

        @pl.when(chain)
        def _():
            hi, lo = split2(xbuf[i])
            a = nt(jnp.concatenate([hi, lo], axis=0), mhi[...])
            a = a[:CD] + a[CD:] + nt(hi, mlo[...])
            part_copy(i).wait_recv()
            obuf[i] = pbuf[i] - a
            send_out(i)

        @pl.when(sol_src)
        def _():
            for d in range(COLS):
                @pl.when(d != c)
                def _():
                    s_copy(i, d).start()
            lane = pl.multiple_of((r % 2) * 512 + (c // 2) * 128, 128)
            sol_ref[i] = xbuf[i, :, pl.ds(lane, 128)]

        @pl.when(jnp.logical_not(chain))
        def _():
            residual(i)

    @pl.when(chain)
    def _():
        @pl.loop(0, CHUNKS)
        def _(i):
            residual(i)

    @pl.loop(0, CHUNKS)
    def _(i):
        @pl.when(jnp.logical_not(sol_src))
        def _():
            s_copy(i, c).wait_recv()
            sol_ref[i] = sbuf[i]

        @pl.loop(0, COLS)
        def _(s):
            @pl.when(s != c)
            def _():
                z_wait(s, i)

        acc = rbuf[0, i]
        for s in range(1, COLS):
            acc = acc + rbuf[s, i]
        res_ref[i] = acc

        @pl.when(jnp.logical_and(late, c < 7))
        def _():
            g_copy(c, i).wait_send()

        for e, (cond, row) in enumerate(edges):
            @pl.when(cond)
            def _():
                x_copy(e, i, row).wait_send()

        @pl.when(produces)
        def _():
            part_copy(i).wait_send()

        @pl.loop(0, COLS)
        def _(d):
            @pl.when(d != c)
            def _():
                z_copy(i, d).wait_send()

                @pl.when(sol_src)
                def _():
                    s_copy(i, d).wait_send()


def body(series, point_order, step_block, panel, diag_inverse):
    dates = series.shape[0]
    ser = jnp.pad(series, ((0, CHUNKS * CD - dates), (0, 0))).reshape(CHUNKS, CD, PIECE)
    idx = point_order.reshape(COLS, PIECE)
    vmem = pl.BlockSpec(memory_space=pltpu.VMEM)
    hbm = pl.BlockSpec(memory_space=pl.ANY)
    dma = pltpu.SemaphoreType.DMA
    res, sol = pl.pallas_call(
        kernel,
        out_shape=(
            jax.ShapeDtypeStruct((CHUNKS, CD, PIECE), F32),
            jax.ShapeDtypeStruct((CHUNKS, CD, 128), F32),
        ),
        in_specs=[pl.BlockSpec(memory_space=pltpu.SMEM), vmem, vmem, hbm, hbm],
        out_specs=(vmem, vmem),
        scratch_shapes=[
            pltpu.VMEM((2 * BS, BS), F32),
            pltpu.VMEM((2 * BS, BS), F32),
            pltpu.VMEM((2 * BS, BS), BF16),
            pltpu.VMEM((2 * BS, BS), BF16),
            pltpu.VMEM((BS, BS), BF16),
            pltpu.VMEM((BS, BS), BF16),
            pltpu.VMEM((BS, BS), BF16),
            pltpu.VMEM((BS, BS), BF16),
            pltpu.VMEM((2 * BS, BS), BF16),
            pltpu.VMEM((COLS, PIECE, PIECE), BF16),
            pltpu.VMEM((7, CHUNKS, CD, PIECE), F32),
            pltpu.VMEM((CHUNKS, CD, BS), F32),
            pltpu.VMEM((CHUNKS, CD, BS), F32),
            pltpu.VMEM((CHUNKS, CD, BS), F32),
            pltpu.VMEM((CHUNKS, COLS, CD, PIECE), F32),
            pltpu.VMEM((COLS, CHUNKS, CD, PIECE), F32),
            pltpu.VMEM((CHUNKS, CD, 128), F32),
            dma((8,)),
            dma((8,)),
            dma((CHUNKS,)),
            dma((7, CHUNKS)),
            dma((4, CHUNKS)),
            dma((CHUNKS,)),
            dma((CHUNKS,)),
            dma((CHUNKS,)),
            dma((CHUNKS, COLS)),
            dma((COLS, CHUNKS)),
            dma((CHUNKS, COLS)),
            dma((CHUNKS,)),
        ],
        compiler_params=pltpu.CompilerParams(
            collective_id=0, has_side_effects=True, vmem_limit_bytes=60 * 1024 * 1024
        ),
    )(step_block, idx, ser, panel, diag_inverse)
    residual = res.reshape(CHUNKS * CD, PIECE)[:dates].T
    half = lax.dynamic_slice_in_dim(sol, lax.axis_index("cols") % 2 * 64, 64, 2)
    solved = half.reshape(CHUNKS * CD, 64)[:dates].T
    return solved, residual


def solution(mesh):
    in_specs = (P(None, ("rows", "cols")), P("rows"), P(), P("rows", "cols"), P("rows", None))
    out_specs = (P(("rows", "cols"), None), P(("rows", "cols"), None))
    return jax.shard_map(body, mesh=mesh, in_specs=in_specs, out_specs=out_specs, check_vma=False)
```

```python
import jax
import jax.numpy as jnp
from jax import lax
from jax.experimental import pallas as pl
from jax.experimental.pallas import tpu as pltpu
from jax.sharding import PartitionSpec as P

MESH = pl.DeviceIdType.MESH
F32 = jnp.float32
BF16 = jnp.bfloat16
DATES = 300
CHUNKS = 10
CD = 32
PAIRS = CHUNKS // 2
PD = 2 * CD
ALL = CHUNKS * CD
BS = 1024
COLS = 8
CHIPS = 4
PIECE = 256
FIRST = 8


def split2(v):
    hi = v.astype(BF16)
    return hi, (v - hi.astype(F32)).astype(BF16)


def split3(v):
    hi = v.astype(BF16)
    rest = v - hi.astype(F32)
    mid = rest.astype(BF16)
    return hi, mid, (rest - mid.astype(F32)).astype(BF16)


def nn(a, b):
    return lax.dot_general(a, b, (((1,), (0,)), ((), ())), preferred_element_type=F32)


def times(hi, lo, weight_hi, weight_lo):
    n = hi.shape[0]
    a = nn(jnp.concatenate([hi, lo], axis=0), weight_hi)
    return a[:n] + (a[n:] + nn(hi, weight_lo))


def span(j, size):
    return pl.ds(pl.multiple_of(j * size, size), size)


def kernel(step_ref, idx_ref, ser_ref, panel_ref, diag_ref, res_ref, sol_ref,
           pf, df, phi, plo, mhi, mlo, dhi, dlo, oh, ohr, serp, gbuf, xbuf, pbuf, obuf, zbuf, zin, rbuf, sbuf,
           pl_sem, dl_sem, gs_sem, gr_sem, f_sem, x_sem, o_sem, p_sem, zs_sem, zr_sem, hs_sem, hr_sem, ss_sem, sr_sem):
    r = lax.axis_index("rows")
    c = lax.axis_index("cols")
    k = r - FIRST
    y, z = r // 4, r % 4
    chip, core = c // 2, c % 2
    root = FIRST + 1 + jnp.minimum(c, 6)
    dy = (y - root // 4 + 4) % 4
    dz = (z - root % 4 + 4) % 4
    late = r >= FIRST
    chain = jnp.logical_and(late, c < k)
    starts = jnp.logical_and(late, c == 7)
    gives = jnp.logical_and(late, c < 7)
    uses_d = jnp.logical_or(chain, starts)
    two = jnp.logical_and(chain, k == 1)
    bulk = jnp.logical_and(late, 2 * chip < k)
    final = jnp.logical_and(late, c == (k + 15) % 8)
    diag_src = jnp.logical_and(final, r < 15)
    diag_dst = jnp.logical_and(c < 7, r == root)
    out_row = jnp.minimum(r + 1, 15)
    prev_col = (c + 7) % 8
    next_col = (c + 1) % 8
    sol_src = c == r // 2

    zp, zm = y * 4 + (z + 1) % 4, y * 4 + (z + 3) % 4
    yp, ym = ((y + 1) % 4) * 4 + z, ((y + 3) % 4) * 4 + z

    barrier = pltpu.get_barrier_semaphore()
    for other in (zp, zm, yp, ym):
        pl.semaphore_signal(barrier, inc=1, device_id=(other, c), device_id_type=MESH)
    for d in range(1, COLS):
        pl.semaphore_signal(barrier, inc=1, device_id=(r, (c + d) % COLS), device_id_type=MESH)

    @pl.when(diag_src)
    def _():
        pl.semaphore_signal(barrier, inc=1, device_id=(out_row, k), device_id_type=MESH)

    @pl.when(diag_dst)
    def _():
        pl.semaphore_signal(barrier, inc=1, device_id=(r - 1, prev_col), device_id_type=MESH)

    def load_d(j):
        rows = span(j, PIECE)
        return pltpu.make_async_copy(diag_ref.at[rows], df.at[rows], dl_sem.at[j])

    def load_p(j):
        rows = span(j, PIECE)
        return pltpu.make_async_copy(panel_ref.at[rows], pf.at[rows], pl_sem.at[j])

    @pl.when(uses_d)
    def _():
        for j in range(8):
            load_d(j).start()

    for j in range(8):
        load_p(j).start()

    whole = DATES // CD * CD
    serp[:whole, :] = ser_ref[:whole, :]
    serp[whole:, :] = jnp.concatenate(
        [ser_ref[whole:, :], jnp.zeros((ALL - DATES, PIECE), F32)], axis=0)

    pl.semaphore_wait(barrier, 11 + diag_src.astype(jnp.int32) + diag_dst.astype(jnp.int32))

    def remote(src, dst, send, recv, device):
        return pltpu.make_async_remote_copy(
            src_ref=src, dst_ref=dst, send_sem=send, recv_sem=recv, device_id=device, device_id_type=MESH)

    def g_copy(src, i):
        return remote(serp.at[span(i, CD)], gbuf.at[src, i], gs_sem.at[i], gr_sem.at[src, i], (r, 7))

    def x_copy(e, i, row):
        part = xbuf.at[span(i, CD)]
        return remote(part, part, f_sem.at[e, i], x_sem.at[i], (row, c))

    def out_copy(i):
        return remote(obuf.at[i], xbuf.at[span(i, CD)], o_sem.at[i], x_sem.at[i], (out_row, k))

    def part_copy(i):
        return remote(obuf.at[i], pbuf.at[i], o_sem.at[i], p_sem.at[i], (r, next_col))

    def hand_copy(p, h):
        return remote(zbuf.at[p, h], zin.at[p, h], hs_sem.at[p, h], hr_sem.at[p, h], (r, c + 1 - 2 * core))

    def z_copy(p, h, q):
        return remote(zbuf.at[p, h, q], rbuf.at[chip, p], zs_sem.at[p, h, q], zr_sem.at[chip, p], (r, 4 * h + q))

    def z_wait(src, p):
        remote(zbuf.at[p, 0, 0], rbuf.at[src, p], zs_sem.at[p, 0, 0], zr_sem.at[src, p], (r, 2 * src + 1)).wait_recv()

    def s_copy(d):
        lane = pl.multiple_of((r % 2) * 512 + (d // 2) * 128, 128)
        return remote(xbuf.at[:, pl.ds(lane, 128)], sbuf, ss_sem.at[d], sr_sem, (r, d))

    edges = (
        (jnp.logical_and(dy == 0, dz <= 1), zp),
        (jnp.logical_and(dy == 0, dz == 0), zm),
        (dy <= 1, yp),
        (dy == 0, ym),
    )

    def send_out(i):
        @pl.when(final)
        def _():
            out_copy(i).start()

        @pl.when(jnp.logical_not(final))
        def _():
            part_copy(i).start()

    @pl.when(gives)
    def _():
        @pl.loop(0, CHUNKS)
        def _(i):
            g_copy(c, i).start()

    slot = step_ref[jnp.maximum(k, 0)] - 2 * r
    shift = r * (COLS * PIECE)

    def pick(first, second):
        return jnp.where(jnp.full(first.shape, slot, jnp.int32) == 0, first, second)

    def pick_rows(ref, j, size):
        return pick(ref[span(j, size), :], ref[pl.ds(pl.multiple_of(BS + j * size, size), size), :])

    def one_hot(row, first):
        pos = lax.broadcasted_iota(jnp.int32, (PIECE, 128), 0) + first
        return jnp.where(pos == row - shift, 1.0, 0.0).astype(BF16)

    @pl.when(uses_d)
    def _():
        @pl.loop(0, 8)
        def _(j):
            load_d(j).wait()

    @pl.when(jnp.logical_or(starts, two))
    def _():
        @pl.loop(0, 8)
        def _(j):
            hi, lo = split2(pick_rows(df, j, 128).T)
            dhi[:, span(j, 128)] = hi
            dlo[:, span(j, 128)] = lo

    @pl.when(starts)
    def _():
        for q in range(8):
            want = pick(idx_ref[q:q + 1, :], idx_ref[8 + q:9 + q, :])

            @pl.loop(0, COLS)
            def _(s):
                oh[span(s, PIECE), q * 128:(q + 1) * 128] = one_hot(want, s * PIECE)

        @pl.loop(0, CHUNKS)
        def _(i):
            hi, lo = split2(serp[span(i, CD), :])
            acc = nn(jnp.concatenate([hi, lo], axis=0), oh[7 * PIECE:, :])
            for s in range(7):
                g_copy(s, i).wait_recv()
                hi, lo = split2(gbuf[s, i])
                acc = acc + nn(jnp.concatenate([hi, lo], axis=0), oh[s * PIECE:(s + 1) * PIECE, :])

            @pl.when(k == 1)
            def _():
                obuf[i] = acc[:CD] + acc[CD:]

            @pl.when(k != 1)
            def _():
                both = acc.astype(BF16)
                obuf[i] = times(both[:CD], both[CD:], dhi[...], dlo[...])

            send_out(i)

    @pl.loop(0, 8)
    def _(j):
        load_p(j).wait()

    def turn_panel():
        @pl.loop(0, 8)
        def _(j):
            hi, lo = split2(pf[span(j, PIECE), :].T)
            phi[:, span(j, PIECE)] = hi
            plo[:, span(j, PIECE)] = lo

    @pl.when(jnp.logical_not(chain))
    def _():
        turn_panel()

    @pl.when(two)
    def _():
        @pl.loop(0, 8)
        def _(j):
            hi, lo = split2(pick_rows(pf, j, 128).T)
            mhi[:, span(j, 128)] = hi
            mlo[:, span(j, 128)] = lo

    @pl.when(jnp.logical_and(chain, k != 1))
    def _():
        @pl.loop(0, 8)
        def _(j):
            rows = span(j, 128)
            hi, lo = split2(pick_rows(df, j, 128))
            dhi[rows, :] = hi
            dlo[rows, :] = lo
            hi, lo = split2(pick_rows(pf, j, 128))
            oh[rows, :] = hi
            oh[pl.ds(pl.multiple_of(BS + j * 128, 128), 128), :] = lo

        @pl.loop(0, 4)
        def _(j):
            rows = span(j, PIECE)
            th = dhi[rows, :]
            ph = oh[:BS, :]
            m = nn(th, ph) + nn(dlo[rows, :], ph) + nn(th, oh[BS:, :])
            hi, lo = split2(m.T)
            mhi[:, rows] = hi
            mlo[:, rows] = lo

    for q in range(16):
        ohr[q // 2, :, q % 2 * 128:(q % 2 + 1) * 128] = one_hot(idx_ref[q:q + 1, :], c * PIECE)

    def half(p, h):
        hi, lo = split2(xbuf[span(p, PD), :])
        three = jnp.concatenate(split3(serp[span(p, PD), :]), axis=0)

        @pl.when(core == 1)
        def _():
            hand_copy(p, h).wait_recv()

        for q in range(4):
            d = 4 * h + q
            cols = span(d, PIECE)
            a = times(hi, lo, phi[:, cols], plo[:, cols])
            b = nn(three, ohr[d])
            v = b[:PD] + (b[PD:2 * PD] + b[2 * PD:]) - a

            @pl.when(core == 0)
            def _():
                zbuf[p, h, q] = v

            @pl.when(core == 1)
            def _():
                total = v + zin[p, h, q]

                @pl.when(d == c)
                def _():
                    rbuf[chip, p] = total

                @pl.when(d != c)
                def _():
                    zbuf[p, h, q] = total
                    z_copy(p, h, q).start()

        @pl.when(core == 0)
        def _():
            hand_copy(p, h).start()

    def arrive(i):
        x_copy(0, i, zp).wait_recv()
        for e, (cond, row) in enumerate(edges):
            @pl.when(cond)
            def _():
                x_copy(e, i, row).start()

    @pl.when(bulk)
    def _():
        @pl.loop(0, CHUNKS)
        def _(i):
            arrive(i)

            @pl.when(chain)
            def _():
                hi, lo = split2(xbuf[span(i, CD), :])
                a = times(hi, lo, mhi[...], mlo[...])
                part_copy(i).wait_recv()
                v = pbuf[i] - a

                @pl.when(two)
                def _():
                    vh, vl = split2(v)
                    obuf[i] = times(vh, vl, dhi[...], dlo[...])

                @pl.when(jnp.logical_not(two))
                def _():
                    obuf[i] = v

                send_out(i)

        @pl.when(chain)
        def _():
            turn_panel()

        @pl.loop(0, CHUNKS)
        def _(i):
            half(i // 2, i % 2)

    @pl.when(jnp.logical_not(bulk))
    def _():
        @pl.loop(0, CHUNKS + 2)
        def _(i):
            @pl.when(i < CHUNKS)
            def _():
                arrive(i)

            @pl.when(i >= 2)
            def _():
                half(i // 2 - 1, i % 2)

    def put_solved(v):
        t = v.T
        sol_ref[...] = jnp.where(jnp.full((64, DATES), core, jnp.int32) == 1, t[64:, :DATES], t[:64, :DATES])

    @pl.when(sol_src)
    def _():
        for d in range(COLS):
            @pl.when(d != c)
            def _():
                s_copy(d).start()
        lane = pl.multiple_of((r % 2) * 512 + chip * 128, 128)
        put_solved(xbuf[:, pl.ds(lane, 128)])

    @pl.when(jnp.logical_not(sol_src))
    def _():
        s_copy(c).wait_recv()
        put_solved(sbuf[...])

    @pl.loop(0, CHIPS)
    def _(s):
        @pl.when(jnp.logical_not(jnp.logical_and(core == 1, s == chip)))
        def _():
            @pl.loop(0, PAIRS)
            def _(p):
                z_wait(s, p)

    total = (rbuf[0] + rbuf[1]) + (rbuf[2] + rbuf[3])
    res_ref[...] = total.reshape(ALL, PIECE)[:DATES, :]

    @pl.loop(0, CHUNKS)
    def _(i):
        @pl.when(gives)
        def _():
            g_copy(c, i).wait_send()

        for e, (cond, row) in enumerate(edges):
            @pl.when(cond)
            def _():
                x_copy(e, i, row).wait_send()

        @pl.when(uses_d)
        def _():
            part_copy(i).wait_send()

        @pl.when(core == 0)
        def _():
            hand_copy(i // 2, i % 2).wait_send()

        @pl.when(core == 1)
        def _():
            for q in range(4):
                @pl.when(4 * (i % 2) + q != c)
                def _():
                    z_copy(i // 2, i % 2, q).wait_send()

    @pl.when(sol_src)
    def _():
        for d in range(COLS):
            @pl.when(d != c)
            def _():
                s_copy(d).wait_send()


def body(series, point_order, step_block, panel, diag_inverse):
    idx = point_order.reshape(16, 128)
    vmem = pl.BlockSpec(memory_space=pltpu.VMEM)
    hbm = pl.BlockSpec(memory_space=pl.ANY)
    dma = pltpu.SemaphoreType.DMA
    residual, solved = pl.pallas_call(
        kernel,
        out_shape=(
            jax.ShapeDtypeStruct((DATES, PIECE), F32),
            jax.ShapeDtypeStruct((64, DATES), F32),
        ),
        in_specs=[pl.BlockSpec(memory_space=pltpu.SMEM), vmem, vmem, hbm, hbm],
        out_specs=(vmem, vmem),
        scratch_shapes=[
            pltpu.VMEM((2 * BS, BS), F32),
            pltpu.VMEM((2 * BS, BS), F32),
            pltpu.VMEM((BS, 2 * BS), BF16),
            pltpu.VMEM((BS, 2 * BS), BF16),
            pltpu.VMEM((BS, BS), BF16),
            pltpu.VMEM((BS, BS), BF16),
            pltpu.VMEM((BS, BS), BF16),
            pltpu.VMEM((BS, BS), BF16),
            pltpu.VMEM((2 * BS, BS), BF16),
            pltpu.VMEM((COLS, PIECE, PIECE), BF16),
            pltpu.VMEM((ALL, PIECE), F32),
            pltpu.VMEM((7, CHUNKS, CD, PIECE), F32),
            pltpu.VMEM((ALL, BS), F32),
            pltpu.VMEM((CHUNKS, CD, BS), F32),
            pltpu.VMEM((CHUNKS, CD, BS), F32),
            pltpu.VMEM((PAIRS, 2, 4, PD, PIECE), F32),
            pltpu.VMEM((PAIRS, 2, 4, PD, PIECE), F32),
            pltpu.VMEM((CHIPS, PAIRS, PD, PIECE), F32),
            pltpu.VMEM((ALL, 128), F32),
            dma((8,)),
            dma((8,)),
            dma((CHUNKS,)),
            dma((7, CHUNKS)),
            dma((4, CHUNKS)),
            dma((CHUNKS,)),
            dma((CHUNKS,)),
            dma((CHUNKS,)),
            dma((PAIRS, 2, 4)),
            dma((CHIPS, PAIRS)),
            dma((PAIRS, 2)),
            dma((PAIRS, 2)),
            dma((COLS,)),
            dma,
        ],
        compiler_params=pltpu.CompilerParams(
            collective_id=0, has_side_effects=True, vmem_limit_bytes=60 * 1024 * 1024
        ),
    )(step_block, idx, series, panel, diag_inverse)
    return solved, residual.T


def solution(mesh):
    in_specs = (P(None, ("rows", "cols")), P("rows"), P(), P("rows", "cols"), P("rows", None))
    out_specs = (P(("rows", "cols"), None), P(("rows", "cols"), None))
    return jax.shard_map(body, mesh=mesh, in_specs=in_specs, out_specs=out_specs, check_vma=False)
```

```python
import jax
import jax.numpy as jnp
from jax import lax
from jax.experimental import pallas as pl
from jax.experimental.pallas import tpu as pltpu
from jax.sharding import PartitionSpec as P

MESH = pl.DeviceIdType.MESH
F32 = jnp.float32
BF16 = jnp.bfloat16
DATES = 300
CHUNKS = 10
CD = 32
PAIRS = CHUNKS // 2
PD = 2 * CD
ALL = CHUNKS * CD
BS = 1024
COLS = 8
CHIPS = 4
PIECE = 256
FIRST = 8


def split2(v):
    hi = v.astype(BF16)
    return hi, (v - hi.astype(F32)).astype(BF16)


def split3(v):
    hi = v.astype(BF16)
    rest = v - hi.astype(F32)
    mid = rest.astype(BF16)
    return hi, mid, (rest - mid.astype(F32)).astype(BF16)


def nn(a, b):
    return lax.dot_general(a, b, (((1,), (0,)), ((), ())), preferred_element_type=F32)


def times(hi, lo, weight_hi, weight_lo):
    n = hi.shape[0]
    a = nn(jnp.concatenate([hi, lo], axis=0), weight_hi)
    return a[:n] + (a[n:] + nn(hi, weight_lo))


def span(j, size):
    return pl.ds(pl.multiple_of(j * size, size), size)


def kernel(step_ref, idx_ref, ser_ref, panel_ref, diag_ref, res_ref, sol_ref,
           pf, df, phi, plo, mhi, mlo, dhi, dlo, oh, ohr, serp, gbuf, xbuf, pin, abuf, obuf, zbuf, zin, rbuf, sbuf,
           pl_sem, dl_sem, gs_sem, gr_sem, f_sem, x_sem, o_sem, far_sem, p_sem, a_sem, zs_sem, zr_sem, hs_sem, hr_sem, ss_sem, sr_sem):
    r = lax.axis_index("rows")
    c = lax.axis_index("cols")
    k = r - FIRST
    y, z = r // 4, r % 4
    chip, core = c // 2, c % 2
    root = FIRST + 1 + jnp.minimum(c, 6)
    dy = (y - root // 4 + 4) % 4
    dz = (z - root % 4 + 4) % 4
    late = r >= FIRST
    chain = jnp.logical_and(late, c < k)
    starts = jnp.logical_and(late, c == 7)
    gives = jnp.logical_and(late, c < 7)
    uses_d = jnp.logical_or(chain, starts)
    bulk = jnp.logical_and(late, 2 * chip < k)
    final = jnp.logical_and(late, c == (k + 15) % 8)
    diag_src = jnp.logical_and(final, r < 15)
    diag_dst = jnp.logical_and(c < 7, r == root)
    far_src = jnp.logical_and(final, r < 14)
    far_dst = jnp.logical_and(c < 6, r == root + 1)
    far_row = jnp.minimum(r + 2, 15)
    solver = jnp.maximum(k - 1, 0)
    out_row = jnp.minimum(r + 1, 15)
    prev_col = (c + 7) % 8
    sol_src = c == r // 2

    zp, zm = y * 4 + (z + 1) % 4, y * 4 + (z + 3) % 4
    yp, ym = ((y + 1) % 4) * 4 + z, ((y + 3) % 4) * 4 + z

    barrier = pltpu.get_barrier_semaphore()
    for other in (zp, zm, yp, ym):
        pl.semaphore_signal(barrier, inc=1, device_id=(other, c), device_id_type=MESH)
    for d in range(1, COLS):
        pl.semaphore_signal(barrier, inc=1, device_id=(r, (c + d) % COLS), device_id_type=MESH)

    @pl.when(diag_src)
    def _():
        pl.semaphore_signal(barrier, inc=1, device_id=(out_row, k), device_id_type=MESH)

    @pl.when(diag_dst)
    def _():
        pl.semaphore_signal(barrier, inc=1, device_id=(r - 1, prev_col), device_id_type=MESH)

    @pl.when(far_src)
    def _():
        pl.semaphore_signal(barrier, inc=1, device_id=(far_row, k), device_id_type=MESH)

    @pl.when(far_dst)
    def _():
        pl.semaphore_signal(barrier, inc=1, device_id=(r - 2, prev_col), device_id_type=MESH)

    def load_d(j):
        rows = span(j, PIECE)
        return pltpu.make_async_copy(diag_ref.at[rows], df.at[rows], dl_sem.at[j])

    def load_p(j):
        rows = span(j, PIECE)
        return pltpu.make_async_copy(panel_ref.at[rows], pf.at[rows], pl_sem.at[j])

    @pl.when(uses_d)
    def _():
        for j in range(8):
            load_d(j).start()

    for j in range(8):
        load_p(j).start()

    whole = DATES // CD * CD
    serp[:whole, :] = ser_ref[:whole, :]
    serp[whole:, :] = jnp.concatenate(
        [ser_ref[whole:, :], jnp.zeros((ALL - DATES, PIECE), F32)], axis=0)

    one = jnp.int32(1)
    zero = jnp.int32(0)
    extra = sum(jnp.where(cond, one, zero) for cond in (diag_src, diag_dst, far_src, far_dst))
    pl.semaphore_wait(barrier, 11 + extra)

    def remote(src, dst, send, recv, device):
        return pltpu.make_async_remote_copy(
            src_ref=src, dst_ref=dst, send_sem=send, recv_sem=recv, device_id=device, device_id_type=MESH)

    def g_copy(src, i):
        return remote(serp.at[span(i, CD)], gbuf.at[src, span(i, CD)], gs_sem.at[i], gr_sem.at[src, i], (r, 7))

    def x_copy(e, i, row):
        part = xbuf.at[span(i, CD)]
        return remote(part, part, f_sem.at[e, i], x_sem.at[i], (row, c))

    def out_copy(i):
        return remote(obuf.at[i], xbuf.at[span(i, CD)], o_sem.at[i], x_sem.at[i], (out_row, k))

    def far_copy(i):
        return remote(obuf.at[i], xbuf.at[span(i, CD)], far_sem.at[i], x_sem.at[i], (far_row, k))

    def pair_copy(i):
        return remote(obuf.at[i], pin.at[i], o_sem.at[i], p_sem.at[i], (r, c + 1 - 2 * core))

    def sum_copy(s, i):
        return remote(obuf.at[i], abuf.at[s, i], o_sem.at[i], a_sem.at[s, i], (r, solver))

    def hand_copy(p, h):
        return remote(zbuf.at[p, h], zin.at[p, h], hs_sem.at[p, h], hr_sem.at[p, h], (r, c + 1 - 2 * core))

    def z_copy(p, h, q):
        return remote(zbuf.at[p, h, q], rbuf.at[chip, p], zs_sem.at[p, h, q], zr_sem.at[chip, p], (r, 4 * h + q))

    def z_wait(src, p):
        remote(zbuf.at[p, 0, 0], rbuf.at[src, p], zs_sem.at[p, 0, 0], zr_sem.at[src, p], (r, 2 * src + 1)).wait_recv()

    def s_copy(d):
        lane = pl.multiple_of((r % 2) * 512 + (d // 2) * 128, 128)
        return remote(xbuf.at[:, pl.ds(lane, 128)], sbuf, ss_sem.at[d], sr_sem, (r, d))

    skip_z = jnp.logical_and(r == root, jnp.logical_and(c < 6, c != 2))
    skip_y = jnp.logical_and(r == FIRST, c == 2)
    edges = (
        (jnp.logical_and(jnp.logical_and(dy == 0, dz <= 1), jnp.logical_not(skip_z)), zp),
        (jnp.logical_and(dy == 0, dz == 0), zm),
        (jnp.logical_and(dy <= 1, jnp.logical_not(skip_y)), yp),
        (dy == 0, ym),
    )

    def send_out(i):
        @pl.when(final)
        def _():
            out_copy(i).start()

            @pl.when(far_src)
            def _():
                far_copy(i).start()

        @pl.when(jnp.logical_not(final))
        def _():
            @pl.when(jnp.logical_and(chain, core == 0))
            def _():
                pair_copy(i).start()

            @pl.when(core == 1)
            def _():
                sum_copy(chip, i).start()

    @pl.when(gives)
    def _():
        @pl.loop(0, CHUNKS)
        def _(i):
            g_copy(c, i).start()

    slot = step_ref[jnp.maximum(k, 0)] - 2 * r
    shift = r * (COLS * PIECE)

    def pick(first, second):
        return jnp.where(jnp.full(first.shape, slot, jnp.int32) == 0, first, second)

    def pick_rows(ref, j, size):
        return pick(ref[span(j, size), :], ref[pl.ds(pl.multiple_of(BS + j * size, size), size), :])

    def one_hot(row, first):
        pos = lax.broadcasted_iota(jnp.int32, (PIECE, 128), 0) + first
        return jnp.where(pos == row - shift, 1.0, 0.0).astype(BF16)

    @pl.when(uses_d)
    def _():
        @pl.loop(0, 8)
        def _(j):
            load_d(j).wait()

    @pl.when(starts)
    def _():
        @pl.loop(0, 8)
        def _(j):
            hi, lo = split2(pick_rows(df, j, 128).T)
            dhi[:, span(j, 128)] = hi
            dlo[:, span(j, 128)] = lo

    @pl.when(starts)
    def _():
        for q in range(8):
            want = pick(idx_ref[q:q + 1, :], idx_ref[8 + q:9 + q, :])

            @pl.loop(0, COLS)
            def _(s):
                oh[span(s, PIECE), q * 128:(q + 1) * 128] = one_hot(want, s * PIECE)

        @pl.loop(0, PAIRS)
        def _(p):
            hi, lo = split2(serp[span(p, PD), :])
            acc = nn(jnp.concatenate([hi, lo], axis=0), oh[7 * PIECE:, :])
            for s in range(7):
                g_copy(s, 2 * p).wait_recv()
                g_copy(s, 2 * p + 1).wait_recv()
                hi, lo = split2(gbuf[s, span(p, PD), :])
                acc = acc + nn(jnp.concatenate([hi, lo], axis=0), oh[s * PIECE:(s + 1) * PIECE, :])
            both = acc.astype(BF16)
            v = times(both[:PD], both[PD:], dhi[...], dlo[...])
            obuf[2 * p] = v[:CD]
            obuf[2 * p + 1] = v[CD:]
            send_out(2 * p)
            send_out(2 * p + 1)

    @pl.loop(0, 8)
    def _(j):
        load_p(j).wait()

    def turn_panel():
        @pl.loop(0, 8)
        def _(j):
            hi, lo = split2(pf[span(j, PIECE), :].T)
            phi[:, span(j, PIECE)] = hi
            plo[:, span(j, PIECE)] = lo

    @pl.when(chain)
    def _():
        @pl.loop(0, 8)
        def _(j):
            rows = span(j, 128)
            hi, lo = split2(pick_rows(df, j, 128))
            dhi[rows, :] = hi
            dlo[rows, :] = lo
            hi, lo = split2(pick_rows(pf, j, 128))
            oh[rows, :] = hi
            oh[pl.ds(pl.multiple_of(BS + j * 128, 128), 128), :] = lo

        @pl.loop(0, 4)
        def _(j):
            rows = span(j, PIECE)
            th = dhi[rows, :]
            ph = oh[:BS, :]
            m = nn(th, ph) + nn(dlo[rows, :], ph) + nn(th, oh[BS:, :])
            hi, lo = split2(m.T)
            mhi[:, rows] = hi
            mlo[:, rows] = lo

    late_turn = jnp.logical_and(chain, k <= 2)

    @pl.when(jnp.logical_not(late_turn))
    def _():
        turn_panel()

    for q in range(16):
        ohr[q // 2, :, q % 2 * 128:(q % 2 + 1) * 128] = one_hot(idx_ref[q:q + 1, :], c * PIECE)

    def half(p, h):
        hi, lo = split2(xbuf[span(p, PD), :])
        three = jnp.concatenate(split3(serp[span(p, PD), :]), axis=0)

        @pl.when(core == 1)
        def _():
            hand_copy(p, h).wait_recv()

        for q in range(4):
            d = 4 * h + q
            cols = span(d, PIECE)
            a = times(hi, lo, phi[:, cols], plo[:, cols])
            b = nn(three, ohr[d])
            v = b[:PD] + (b[PD:2 * PD] + b[2 * PD:]) - a

            @pl.when(core == 0)
            def _():
                zbuf[p, h, q] = v

            @pl.when(core == 1)
            def _():
                total = v + zin[p, h, q]

                @pl.when(d == c)
                def _():
                    rbuf[chip, p] = total

                @pl.when(d != c)
                def _():
                    zbuf[p, h, q] = total
                    z_copy(p, h, q).start()

        @pl.when(core == 0)
        def _():
            hand_copy(p, h).start()

    def arrive(i):
        x_copy(0, i, zp).wait_recv()

    def forward(i):
        for e, (cond, row) in enumerate(edges):
            @pl.when(cond)
            def _():
                x_copy(e, i, row).start()

    solves = jnp.logical_and(chain, final)

    @pl.when(bulk)
    def _():
        @pl.loop(0, CHUNKS)
        def _(i):
            arrive(i)

            @pl.when(jnp.logical_not(solves))
            def _():
                forward(i)

            @pl.when(chain)
            def _():
                hi, lo = split2(xbuf[span(i, CD), :])
                obuf[i] = times(hi, lo, mhi[...], mlo[...])

                @pl.when(core == 1)
                def _():
                    pair_copy(i).wait_recv()
                    obuf[i] = obuf[i] + pin[i]

                @pl.when(final)
                def _():
                    for s in range(CHIPS - 1):
                        @pl.when(s < chip)
                        def _():
                            sum_copy(s, i).wait_recv()
                            obuf[i] = obuf[i] + abuf[s, i]
                    sum_copy(3, i).wait_recv()
                    obuf[i] = abuf[3, i] - obuf[i]

                send_out(i)

            @pl.when(solves)
            def _():
                forward(i)

        @pl.when(late_turn)
        def _():
            turn_panel()

        @pl.loop(0, CHUNKS)
        def _(i):
            half(i // 2, i % 2)

    @pl.when(jnp.logical_not(bulk))
    def _():
        @pl.loop(0, CHUNKS + 2)
        def _(i):
            @pl.when(i < CHUNKS)
            def _():
                arrive(i)
                forward(i)

            @pl.when(i >= 2)
            def _():
                half(i // 2 - 1, i % 2)

    def put_solved(v):
        t = v.T
        sol_ref[...] = jnp.where(jnp.full((64, DATES), core, jnp.int32) == 1, t[64:, :DATES], t[:64, :DATES])

    @pl.when(sol_src)
    def _():
        for d in range(COLS):
            @pl.when(d != c)
            def _():
                s_copy(d).start()
        lane = pl.multiple_of((r % 2) * 512 + chip * 128, 128)
        put_solved(xbuf[:, pl.ds(lane, 128)])

    @pl.when(jnp.logical_not(sol_src))
    def _():
        s_copy(c).wait_recv()
        put_solved(sbuf[...])

    @pl.loop(0, CHIPS)
    def _(s):
        @pl.when(jnp.logical_not(jnp.logical_and(core == 1, s == chip)))
        def _():
            @pl.loop(0, PAIRS)
            def _(p):
                z_wait(s, p)

    total = (rbuf[0] + rbuf[1]) + (rbuf[2] + rbuf[3])
    res_ref[...] = total.reshape(ALL, PIECE)[:DATES, :]

    @pl.loop(0, CHUNKS)
    def _(i):
        @pl.when(gives)
        def _():
            g_copy(c, i).wait_send()

        for e, (cond, row) in enumerate(edges):
            @pl.when(cond)
            def _():
                x_copy(e, i, row).wait_send()

        @pl.when(uses_d)
        def _():
            pair_copy(i).wait_send()

        @pl.when(far_src)
        def _():
            far_copy(i).wait_send()

        @pl.when(core == 0)
        def _():
            hand_copy(i // 2, i % 2).wait_send()

        @pl.when(core == 1)
        def _():
            for q in range(4):
                @pl.when(4 * (i % 2) + q != c)
                def _():
                    z_copy(i // 2, i % 2, q).wait_send()

    @pl.when(sol_src)
    def _():
        for d in range(COLS):
            @pl.when(d != c)
            def _():
                s_copy(d).wait_send()


def body(series, point_order, step_block, panel, diag_inverse):
    idx = point_order.reshape(16, 128)
    vmem = pl.BlockSpec(memory_space=pltpu.VMEM)
    hbm = pl.BlockSpec(memory_space=pl.ANY)
    dma = pltpu.SemaphoreType.DMA
    residual, solved = pl.pallas_call(
        kernel,
        out_shape=(
            jax.ShapeDtypeStruct((DATES, PIECE), F32),
            jax.ShapeDtypeStruct((64, DATES), F32),
        ),
        in_specs=[pl.BlockSpec(memory_space=pltpu.SMEM), vmem, vmem, hbm, hbm],
        out_specs=(vmem, vmem),
        scratch_shapes=[
            pltpu.VMEM((2 * BS, BS), F32),
            pltpu.VMEM((2 * BS, BS), F32),
            pltpu.VMEM((BS, 2 * BS), BF16),
            pltpu.VMEM((BS, 2 * BS), BF16),
            pltpu.VMEM((BS, BS), BF16),
            pltpu.VMEM((BS, BS), BF16),
            pltpu.VMEM((BS, BS), BF16),
            pltpu.VMEM((BS, BS), BF16),
            pltpu.VMEM((2 * BS, BS), BF16),
            pltpu.VMEM((COLS, PIECE, PIECE), BF16),
            pltpu.VMEM((ALL, PIECE), F32),
            pltpu.VMEM((7, ALL, PIECE), F32),
            pltpu.VMEM((ALL, BS), F32),
            pltpu.VMEM((CHUNKS, CD, BS), F32),
            pltpu.VMEM((CHIPS, CHUNKS, CD, BS), F32),
            pltpu.VMEM((CHUNKS, CD, BS), F32),
            pltpu.VMEM((PAIRS, 2, 4, PD, PIECE), F32),
            pltpu.VMEM((PAIRS, 2, 4, PD, PIECE), F32),
            pltpu.VMEM((CHIPS, PAIRS, PD, PIECE), F32),
            pltpu.VMEM((ALL, 128), F32),
            dma((8,)),
            dma((8,)),
            dma((CHUNKS,)),
            dma((7, CHUNKS)),
            dma((4, CHUNKS)),
            dma((CHUNKS,)),
            dma((CHUNKS,)),
            dma((CHUNKS,)),
            dma((CHUNKS,)),
            dma((CHIPS, CHUNKS)),
            dma((PAIRS, 2, 4)),
            dma((CHIPS, PAIRS)),
            dma((PAIRS, 2)),
            dma((PAIRS, 2)),
            dma((COLS,)),
            dma,
        ],
        compiler_params=pltpu.CompilerParams(
            collective_id=0, has_side_effects=True, vmem_limit_bytes=60 * 1024 * 1024
        ),
    )(step_block, idx, series, panel, diag_inverse)
    return solved, residual.T


def solution(mesh):
    in_specs = (P(None, ("rows", "cols")), P("rows"), P(), P("rows", "cols"), P("rows", None))
    out_specs = (P(("rows", "cols"), None), P(("rows", "cols"), None))
    return jax.shard_map(body, mesh=mesh, in_specs=in_specs, out_specs=out_specs, check_vma=False)
```

```python
import jax
import jax.numpy as jnp
from jax import lax
from jax.experimental import pallas as pl
from jax.experimental.pallas import tpu as pltpu
from jax.sharding import PartitionSpec as P

MESH = pl.DeviceIdType.MESH
F32 = jnp.float32
BF16 = jnp.bfloat16
DATES = 300
CHUNKS = 10
CD = 32
PAIRS = CHUNKS // 2
PD = 2 * CD
ALL = CHUNKS * CD
BS = 1024
COLS = 8
CHIPS = 4
PIECE = 256
FIRST = 8


def split2(v):
    hi = v.astype(BF16)
    return hi, (v - hi.astype(F32)).astype(BF16)


def split3(v):
    hi = v.astype(BF16)
    rest = v - hi.astype(F32)
    mid = rest.astype(BF16)
    return hi, mid, (rest - mid.astype(F32)).astype(BF16)


def nn(a, b):
    return lax.dot_general(a, b, (((1,), (0,)), ((), ())), preferred_element_type=F32)


def times(hi, lo, weight_hi, weight_lo):
    n = hi.shape[0]
    a = nn(jnp.concatenate([hi, lo], axis=0), weight_hi)
    return a[:n] + (a[n:] + nn(hi, weight_lo))


def span(j, size):
    return pl.ds(pl.multiple_of(j * size, size), size)


def kernel(step_ref, idx_ref, ser_ref, panel_ref, diag_ref, res_ref, sol_ref,
           pf, df, phi, plo, mhi, mlo, dhi, dlo, oh, ohr, serp, gbuf, xbuf, pin, abuf, obuf, zbuf, zin, rbuf, sbuf,
           pl_sem, dl_sem, gs_sem, gr_sem, f_sem, x_sem, o_sem, v_sem, p_sem, a_sem, zs_sem, zr_sem, hs_sem, hr_sem, ss_sem, sr_sem):
    r = lax.axis_index("rows")
    c = lax.axis_index("cols")
    k = r - FIRST
    y, z = r // 4, r % 4
    chip, core = c // 2, c % 2
    root = FIRST + 1 + jnp.minimum(c, 6)
    dy = (y - root // 4 + 4) % 4
    dz = (z - root % 4 + 4) % 4
    late = r >= FIRST
    chain = jnp.logical_and(late, c < k)
    starts = jnp.logical_and(late, c == 7)
    gives = jnp.logical_and(late, c < 7)
    uses_d = jnp.logical_or(chain, starts)
    bulk = jnp.logical_and(late, 2 * chip < k)
    final = jnp.logical_and(late, c == (k + 15) % 8)
    diag_src = jnp.logical_and(final, r < 15)
    diag_dst = jnp.logical_and(c < 7, r == root)
    solver = jnp.maximum(k - 1, 0)
    solver_chip = solver // 2
    near = jnp.logical_or(chip + 1 == solver_chip, jnp.logical_or(c == 7, jnp.logical_and(chip == 0, solver_chip == 3)))
    sum_col = jnp.where(near, solver, jnp.minimum(c + 2, 7))
    takes = jnp.logical_and(jnp.logical_and(chain, core == 1), jnp.logical_and(chip >= 1, chip + 1 == solver_chip))
    via_src = jnp.logical_or(jnp.logical_and(r == 8, c == 7), jnp.logical_and(r == 12, c == 3))
    via_dev = jnp.logical_or(jnp.logical_and(r == 10, c == 6), jnp.logical_and(r == 14, c == 7))
    via_row = jnp.minimum(r + 2, 15)
    via_col = jnp.where(r == 8, 6, 7)
    via_from = jnp.where(r == 10, 7, 3)
    via_to = jnp.where(r == 10, 0, 4)
    out_row = jnp.minimum(r + 1, 15)
    prev_col = (c + 7) % 8
    sol_src = c == r // 2

    zp, zm = y * 4 + (z + 1) % 4, y * 4 + (z + 3) % 4
    yp, ym = ((y + 1) % 4) * 4 + z, ((y + 3) % 4) * 4 + z

    barrier = pltpu.get_barrier_semaphore()
    for other in (zp, zm, yp, ym):
        pl.semaphore_signal(barrier, inc=1, device_id=(other, c), device_id_type=MESH)
    for d in range(1, COLS):
        pl.semaphore_signal(barrier, inc=1, device_id=(r, (c + d) % COLS), device_id_type=MESH)

    @pl.when(diag_src)
    def _():
        pl.semaphore_signal(barrier, inc=1, device_id=(out_row, k), device_id_type=MESH)

    @pl.when(diag_dst)
    def _():
        pl.semaphore_signal(barrier, inc=1, device_id=(r - 1, prev_col), device_id_type=MESH)

    @pl.when(via_src)
    def _():
        pl.semaphore_signal(barrier, inc=1, device_id=(via_row, via_col), device_id_type=MESH)

    @pl.when(via_dev)
    def _():
        pl.semaphore_signal(barrier, inc=1, device_id=(jnp.maximum(r - 2, 0), via_from), device_id_type=MESH)

    def load_d(j):
        rows = span(j, PIECE)
        return pltpu.make_async_copy(diag_ref.at[rows], df.at[rows], dl_sem.at[j])

    def load_p(j):
        rows = span(j, PIECE)
        return pltpu.make_async_copy(panel_ref.at[rows], pf.at[rows], pl_sem.at[j])

    @pl.when(uses_d)
    def _():
        for j in range(8):
            load_d(j).start()

    for j in range(8):
        load_p(j).start()

    whole = DATES // CD * CD
    serp[:whole, :] = ser_ref[:whole, :]
    serp[whole:, :] = jnp.concatenate(
        [ser_ref[whole:, :], jnp.zeros((ALL - DATES, PIECE), F32)], axis=0)

    one = jnp.int32(1)
    zero = jnp.int32(0)
    extra = sum(jnp.where(cond, one, zero) for cond in (diag_src, diag_dst, via_src, via_dev))
    pl.semaphore_wait(barrier, 11 + extra)

    def remote(src, dst, send, recv, device):
        return pltpu.make_async_remote_copy(
            src_ref=src, dst_ref=dst, send_sem=send, recv_sem=recv, device_id=device, device_id_type=MESH)

    def g_copy(src, i):
        return remote(serp.at[span(i, CD)], gbuf.at[src, span(i, CD)], gs_sem.at[i], gr_sem.at[src, i], (r, 7))

    def x_copy(e, i, row):
        part = xbuf.at[span(i, CD)]
        return remote(part, part, f_sem.at[e, i], x_sem.at[i], (row, c))

    def out_copy(i):
        return remote(obuf.at[i], xbuf.at[span(i, CD)], o_sem.at[i], x_sem.at[i], (out_row, k))

    def via_copy(i):
        return remote(obuf.at[i], abuf.at[0, i], v_sem.at[i], a_sem.at[0, i], (via_row, via_col))

    def hop_copy(i):
        return remote(abuf.at[0, i], xbuf.at[span(i, CD)], v_sem.at[i], x_sem.at[i], (r, via_to))

    def pair_copy(i):
        return remote(obuf.at[i], pin.at[i], o_sem.at[i], p_sem.at[i], (r, c + 1 - 2 * core))

    def sum_copy(s, i):
        return remote(obuf.at[i], abuf.at[s, i], o_sem.at[i], a_sem.at[s, i], (r, sum_col))

    def hand_copy(p, h):
        return remote(zbuf.at[p, h], zin.at[p, h], hs_sem.at[p, h], hr_sem.at[p, h], (r, c + 1 - 2 * core))

    def z_copy(p, h, q):
        return remote(zbuf.at[p, h, q], rbuf.at[chip, p], zs_sem.at[p, h, q], zr_sem.at[chip, p], (r, 4 * h + q))

    def z_wait(src, p):
        remote(zbuf.at[p, 0, 0], rbuf.at[src, p], zs_sem.at[p, 0, 0], zr_sem.at[src, p], (r, 2 * src + 1)).wait_recv()

    def s_copy(d):
        lane = pl.multiple_of((r % 2) * 512 + (d // 2) * 128, 128)
        return remote(xbuf.at[:, pl.ds(lane, 128)], sbuf, ss_sem.at[d], sr_sem, (r, d))

    turned = c == 7
    on_z = jnp.logical_or(turned, dy == 0)
    on_y = jnp.logical_or(jnp.logical_not(turned), dz == 0)
    served = jnp.logical_and(r == root, jnp.logical_or(c == 0, c == 4))
    edges = (
        (jnp.logical_and(jnp.logical_and(on_z, dz <= 1), jnp.logical_not(served)), zp),
        (jnp.logical_and(on_z, dz == 0), zm),
        (jnp.logical_and(on_y, dy <= 1), yp),
        (jnp.logical_and(on_y, dy == 0), ym),
    )

    def send_out(i):
        @pl.when(final)
        def _():
            out_copy(i).start()

            @pl.when(via_src)
            def _():
                via_copy(i).start()

        @pl.when(jnp.logical_not(final))
        def _():
            @pl.when(jnp.logical_and(chain, core == 0))
            def _():
                pair_copy(i).start()

            @pl.when(core == 1)
            def _():
                sum_copy(chip, i).start()

    @pl.when(gives)
    def _():
        @pl.loop(0, PAIRS)
        def _(p):
            g_copy(c, 2 * p).start()
            g_copy(c, 2 * p + 1).start()

            @pl.when(r == FIRST)
            def _():
                g_copy(c, 2 * p).wait_send()
                g_copy(c, 2 * p + 1).wait_send()

    slot = step_ref[jnp.maximum(k, 0)] - 2 * r
    shift = r * (COLS * PIECE)

    def pick(first, second):
        return jnp.where(jnp.full(first.shape, slot, jnp.int32) == 0, first, second)

    def pick_rows(ref, j, size):
        return pick(ref[span(j, size), :], ref[pl.ds(pl.multiple_of(BS + j * size, size), size), :])

    def one_hot(row, first):
        pos = lax.broadcasted_iota(jnp.int32, (PIECE, 128), 0) + first
        return jnp.where(pos == row - shift, 1.0, 0.0).astype(BF16)

    @pl.when(uses_d)
    def _():
        @pl.loop(0, 8)
        def _(j):
            load_d(j).wait()

    @pl.when(starts)
    def _():
        @pl.loop(0, 8)
        def _(j):
            hi, lo = split2(pick_rows(df, j, 128).T)
            dhi[:, span(j, 128)] = hi
            dlo[:, span(j, 128)] = lo

    @pl.when(starts)
    def _():
        for q in range(8):
            want = pick(idx_ref[q:q + 1, :], idx_ref[8 + q:9 + q, :])

            @pl.loop(0, COLS)
            def _(s):
                oh[span(s, PIECE), q * 128:(q + 1) * 128] = one_hot(want, s * PIECE)

        @pl.loop(0, PAIRS)
        def _(p):
            hi, lo = split2(serp[span(p, PD), :])
            acc = nn(jnp.concatenate([hi, lo], axis=0), oh[7 * PIECE:, :])
            for s in range(7):
                g_copy(s, 2 * p).wait_recv()
                g_copy(s, 2 * p + 1).wait_recv()
                hi, lo = split2(gbuf[s, span(p, PD), :])
                acc = acc + nn(jnp.concatenate([hi, lo], axis=0), oh[s * PIECE:(s + 1) * PIECE, :])
            both = acc.astype(BF16)
            v = times(both[:PD], both[PD:], dhi[...], dlo[...])
            obuf[2 * p] = v[:CD]
            obuf[2 * p + 1] = v[CD:]
            send_out(2 * p)
            send_out(2 * p + 1)

    @pl.loop(0, 8)
    def _(j):
        load_p(j).wait()

    def turn_panel():
        @pl.loop(0, 8)
        def _(j):
            hi, lo = split2(pf[span(j, PIECE), :].T)
            phi[:, span(j, PIECE)] = hi
            plo[:, span(j, PIECE)] = lo

    @pl.when(chain)
    def _():
        @pl.loop(0, 8)
        def _(j):
            rows = span(j, 128)
            hi, lo = split2(pick_rows(df, j, 128))
            dhi[rows, :] = hi
            dlo[rows, :] = lo
            hi, lo = split2(pick_rows(pf, j, 128))
            oh[rows, :] = hi
            oh[pl.ds(pl.multiple_of(BS + j * 128, 128), 128), :] = lo

        @pl.loop(0, 4)
        def _(j):
            rows = span(j, PIECE)
            th = dhi[rows, :]
            ph = oh[:BS, :]
            m = nn(th, ph) + nn(dlo[rows, :], ph) + nn(th, oh[BS:, :])
            hi, lo = split2(m.T)
            mhi[:, rows] = hi
            mlo[:, rows] = lo

    late_turn = jnp.logical_and(chain, k <= 2)

    @pl.when(jnp.logical_not(late_turn))
    def _():
        turn_panel()

    for q in range(16):
        ohr[q // 2, :, q % 2 * 128:(q % 2 + 1) * 128] = one_hot(idx_ref[q:q + 1, :], c * PIECE)

    def half(p, h):
        hi, lo = split2(xbuf[span(p, PD), :])
        three = jnp.concatenate(split3(serp[span(p, PD), :]), axis=0)

        @pl.when(core == 1)
        def _():
            hand_copy(p, h).wait_recv()

        for q in range(4):
            d = 4 * h + q
            cols = span(d, PIECE)
            a = times(hi, lo, phi[:, cols], plo[:, cols])
            b = nn(three, ohr[d])
            v = b[:PD] + (b[PD:2 * PD] + b[2 * PD:]) - a

            @pl.when(core == 0)
            def _():
                zbuf[p, h, q] = v

            @pl.when(core == 1)
            def _():
                total = v + zin[p, h, q]

                @pl.when(d == c)
                def _():
                    rbuf[chip, p] = total

                @pl.when(d != c)
                def _():
                    zbuf[p, h, q] = total
                    z_copy(p, h, q).start()

        @pl.when(core == 0)
        def _():
            hand_copy(p, h).start()

    def arrive(i):
        x_copy(0, i, zp).wait_recv()

    def forward(i, first=0, last=4):
        for e, (cond, row) in list(enumerate(edges))[first:last]:
            @pl.when(cond)
            def _():
                x_copy(e, i, row).start()

    solves = jnp.logical_and(chain, final)

    @pl.when(via_dev)
    def _():
        @pl.loop(0, CHUNKS)
        def _(i):
            sum_copy(0, i).wait_recv()
            hop_copy(i).start()

    @pl.when(bulk)
    def _():
        @pl.loop(0, CHUNKS)
        def _(i):
            arrive(i)

            forward(i, 0, 1)

            @pl.when(jnp.logical_not(solves))
            def _():
                forward(i, 1, 4)

            @pl.when(chain)
            def _():
                hi, lo = split2(xbuf[span(i, CD), :])
                obuf[i] = times(hi, lo, mhi[...], mlo[...])

                @pl.when(core == 1)
                def _():
                    pair_copy(i).wait_recv()
                    obuf[i] = obuf[i] + pin[i]

                @pl.when(takes)
                def _():
                    sum_copy(chip - 1, i).wait_recv()
                    obuf[i] = obuf[i] + abuf[chip - 1, i]

                @pl.when(final)
                def _():
                    for s in range(CHIPS - 1):
                        @pl.when(jnp.logical_or(s == chip - 1, jnp.logical_and(s == 0, chip == 3)))
                        def _():
                            sum_copy(s, i).wait_recv()
                            obuf[i] = obuf[i] + abuf[s, i]
                    sum_copy(3, i).wait_recv()
                    obuf[i] = abuf[3, i] - obuf[i]

                send_out(i)

            @pl.when(solves)
            def _():
                forward(i, 1, 4)

        @pl.when(late_turn)
        def _():
            turn_panel()

        @pl.loop(0, CHUNKS)
        def _(i):
            half(i // 2, i % 2)

    @pl.when(jnp.logical_not(bulk))
    def _():
        @pl.loop(0, CHUNKS + 2)
        def _(i):
            @pl.when(i < CHUNKS)
            def _():
                arrive(i)
                forward(i)

            @pl.when(i >= 2)
            def _():
                half(i // 2 - 1, i % 2)

    def put_solved(v):
        t = v.T
        sol_ref[...] = jnp.where(jnp.full((64, DATES), core, jnp.int32) == 1, t[64:, :DATES], t[:64, :DATES])

    @pl.when(sol_src)
    def _():
        for d in range(COLS):
            @pl.when(d != c)
            def _():
                s_copy(d).start()
        lane = pl.multiple_of((r % 2) * 512 + chip * 128, 128)
        put_solved(xbuf[:, pl.ds(lane, 128)])

    @pl.when(jnp.logical_not(sol_src))
    def _():
        s_copy(c).wait_recv()
        put_solved(sbuf[...])

    @pl.loop(0, CHIPS)
    def _(s):
        @pl.when(jnp.logical_not(jnp.logical_and(core == 1, s == chip)))
        def _():
            @pl.loop(0, PAIRS)
            def _(p):
                z_wait(s, p)

    total = (rbuf[0] + rbuf[1]) + (rbuf[2] + rbuf[3])
    res_ref[...] = total.reshape(ALL, PIECE)[:DATES, :]

    @pl.loop(0, CHUNKS)
    def _(i):
        @pl.when(jnp.logical_and(gives, r != FIRST))
        def _():
            g_copy(c, i).wait_send()

        for e, (cond, row) in enumerate(edges):
            @pl.when(cond)
            def _():
                x_copy(e, i, row).wait_send()

        @pl.when(uses_d)
        def _():
            pair_copy(i).wait_send()

        @pl.when(jnp.logical_or(via_src, via_dev))
        def _():
            via_copy(i).wait_send()

        @pl.when(core == 0)
        def _():
            hand_copy(i // 2, i % 2).wait_send()

        @pl.when(core == 1)
        def _():
            for q in range(4):
                @pl.when(4 * (i % 2) + q != c)
                def _():
                    z_copy(i // 2, i % 2, q).wait_send()

    @pl.when(sol_src)
    def _():
        for d in range(COLS):
            @pl.when(d != c)
            def _():
                s_copy(d).wait_send()


def body(series, point_order, step_block, panel, diag_inverse):
    idx = point_order.reshape(16, 128)
    vmem = pl.BlockSpec(memory_space=pltpu.VMEM)
    hbm = pl.BlockSpec(memory_space=pl.ANY)
    dma = pltpu.SemaphoreType.DMA
    residual, solved = pl.pallas_call(
        kernel,
        out_shape=(
            jax.ShapeDtypeStruct((DATES, PIECE), F32),
            jax.ShapeDtypeStruct((64, DATES), F32),
        ),
        in_specs=[pl.BlockSpec(memory_space=pltpu.SMEM), vmem, vmem, hbm, hbm],
        out_specs=(vmem, vmem),
        scratch_shapes=[
            pltpu.VMEM((2 * BS, BS), F32),
            pltpu.VMEM((2 * BS, BS), F32),
            pltpu.VMEM((BS, 2 * BS), BF16),
            pltpu.VMEM((BS, 2 * BS), BF16),
            pltpu.VMEM((BS, BS), BF16),
            pltpu.VMEM((BS, BS), BF16),
            pltpu.VMEM((BS, BS), BF16),
            pltpu.VMEM((BS, BS), BF16),
            pltpu.VMEM((2 * BS, BS), BF16),
            pltpu.VMEM((COLS, PIECE, PIECE), BF16),
            pltpu.VMEM((ALL, PIECE), F32),
            pltpu.VMEM((7, ALL, PIECE), F32),
            pltpu.VMEM((ALL, BS), F32),
            pltpu.VMEM((CHUNKS, CD, BS), F32),
            pltpu.VMEM((CHIPS, CHUNKS, CD, BS), F32),
            pltpu.VMEM((CHUNKS, CD, BS), F32),
            pltpu.VMEM((PAIRS, 2, 4, PD, PIECE), F32),
            pltpu.VMEM((PAIRS, 2, 4, PD, PIECE), F32),
            pltpu.VMEM((CHIPS, PAIRS, PD, PIECE), F32),
            pltpu.VMEM((ALL, 128), F32),
            dma((8,)),
            dma((8,)),
            dma((CHUNKS,)),
            dma((7, CHUNKS)),
            dma((4, CHUNKS)),
            dma((CHUNKS,)),
            dma((CHUNKS,)),
            dma((CHUNKS,)),
            dma((CHUNKS,)),
            dma((CHIPS, CHUNKS)),
            dma((PAIRS, 2, 4)),
            dma((CHIPS, PAIRS)),
            dma((PAIRS, 2)),
            dma((PAIRS, 2)),
            dma((COLS,)),
            dma,
        ],
        compiler_params=pltpu.CompilerParams(
            collective_id=0, has_side_effects=True, vmem_limit_bytes=60 * 1024 * 1024
        ),
    )(step_block, idx, series, panel, diag_inverse)
    return solved, residual.T


def solution(mesh):
    in_specs = (P(None, ("rows", "cols")), P("rows"), P(), P("rows", "cols"), P("rows", None))
    out_specs = (P(("rows", "cols"), None), P(("rows", "cols"), None))
    return jax.shard_map(body, mesh=mesh, in_specs=in_specs, out_specs=out_specs, check_vma=False)
```

```python
import jax
import jax.numpy as jnp
from jax import lax
from jax.experimental import pallas as pl
from jax.experimental.pallas import tpu as pltpu
from jax.sharding import PartitionSpec as P

MESH = pl.DeviceIdType.MESH
F32 = jnp.float32
BF16 = jnp.bfloat16
DATES = 300
CHUNKS = 10
CD = 32
PAIRS = CHUNKS // 2
PD = 2 * CD
ALL = CHUNKS * CD
BS = 1024
COLS = 8
CHIPS = 4
PIECE = 256
FIRST = 8


def split2(v):
    hi = v.astype(BF16)
    return hi, (v - hi.astype(F32)).astype(BF16)


def split3(v):
    hi = v.astype(BF16)
    rest = v - hi.astype(F32)
    mid = rest.astype(BF16)
    return hi, mid, (rest - mid.astype(F32)).astype(BF16)


def nn(a, b):
    return lax.dot_general(a, b, (((1,), (0,)), ((), ())), preferred_element_type=F32)


def times(hi, lo, weight_hi, weight_lo):
    n = hi.shape[0]
    a = nn(jnp.concatenate([hi, lo], axis=0), weight_hi)
    return a[:n] + (a[n:] + nn(hi, weight_lo))


def span(j, size):
    return pl.ds(pl.multiple_of(j * size, size), size)


def kernel(step_ref, idx_ref, ser_ref, panel_ref, diag_ref, res_ref, sol_ref,
           pf, df, phi, plo, mhi, mlo, dhi, dlo, oh, ohr, serp, gbuf, xbuf, pin, abuf, obuf, zbuf, zin, rbuf, sbuf,
           pl_sem, dl_sem, gs_sem, gr_sem, f_sem, x_sem, o_sem, v_sem, p_sem, a_sem, zs_sem, zr_sem, hs_sem, hr_sem, ss_sem, sr_sem):
    r = lax.axis_index("rows")
    c = lax.axis_index("cols")
    k = r - FIRST
    y, z = r // 4, r % 4
    chip, core = c // 2, c % 2
    root = FIRST + 1 + jnp.minimum(c, 6)
    dy = (y - root // 4 + 4) % 4
    dz = (z - root % 4 + 4) % 4
    late = r >= FIRST
    chain = jnp.logical_and(late, c < k)
    starts = jnp.logical_and(late, c == 7)
    gives = jnp.logical_and(late, c < 7)
    uses_d = jnp.logical_or(chain, starts)
    bulk = jnp.logical_and(late, 2 * chip < k)
    final = jnp.logical_and(late, c == (k + 15) % 8)
    diag_src = jnp.logical_and(final, r < 15)
    diag_dst = jnp.logical_and(c < 7, r == root)
    solver = jnp.maximum(k - 1, 0)
    solver_chip = solver // 2
    near = jnp.logical_or(chip + 1 == solver_chip, jnp.logical_or(c == 7, jnp.logical_and(chip == 0, solver_chip == 3)))
    sum_col = jnp.where(near, solver, jnp.minimum(c + 2, 7))
    takes = jnp.logical_and(jnp.logical_and(chain, core == 1), jnp.logical_and(chip >= 1, chip + 1 == solver_chip))
    via_src = jnp.logical_or(jnp.logical_and(r == 8, c == 7), jnp.logical_and(r == 12, c == 3))
    via_dev = jnp.logical_or(jnp.logical_and(r == 10, c == 6), jnp.logical_and(r == 14, c == 7))
    via_row = jnp.minimum(r + 2, 15)
    via_col = jnp.where(r == 8, 6, 7)
    via_from = jnp.where(r == 10, 7, 3)
    via_to = jnp.where(r == 10, 0, 4)
    out_row = jnp.minimum(r + 1, 15)
    prev_col = (c + 7) % 8
    sol_src = c == r // 2

    zp, zm = y * 4 + (z + 1) % 4, y * 4 + (z + 3) % 4
    yp, ym = ((y + 1) % 4) * 4 + z, ((y + 3) % 4) * 4 + z

    barrier = pltpu.get_barrier_semaphore()
    for other in (zp, zm, yp, ym):
        pl.semaphore_signal(barrier, inc=1, device_id=(other, c), device_id_type=MESH)
    for d in range(1, COLS):
        pl.semaphore_signal(barrier, inc=1, device_id=(r, (c + d) % COLS), device_id_type=MESH)

    @pl.when(diag_src)
    def _():
        pl.semaphore_signal(barrier, inc=1, device_id=(out_row, k), device_id_type=MESH)

    @pl.when(diag_dst)
    def _():
        pl.semaphore_signal(barrier, inc=1, device_id=(r - 1, prev_col), device_id_type=MESH)

    @pl.when(via_src)
    def _():
        pl.semaphore_signal(barrier, inc=1, device_id=(via_row, via_col), device_id_type=MESH)

    @pl.when(via_dev)
    def _():
        pl.semaphore_signal(barrier, inc=1, device_id=(jnp.maximum(r - 2, 0), via_from), device_id_type=MESH)

    def load_d(j):
        rows = span(j, PIECE)
        return pltpu.make_async_copy(diag_ref.at[rows], df.at[rows], dl_sem.at[j])

    def load_p(j):
        rows = span(j, PIECE)
        return pltpu.make_async_copy(panel_ref.at[rows], pf.at[rows], pl_sem.at[j])

    @pl.when(uses_d)
    def _():
        for j in range(8):
            load_d(j).start()

    for j in range(8):
        load_p(j).start()

    whole = DATES // CD * CD
    serp[:whole, :] = ser_ref[:whole, :]
    serp[whole:, :] = jnp.concatenate(
        [ser_ref[whole:, :], jnp.zeros((ALL - DATES, PIECE), F32)], axis=0)

    one = jnp.int32(1)
    zero = jnp.int32(0)
    extra = sum(jnp.where(cond, one, zero) for cond in (diag_src, diag_dst, via_src, via_dev))
    pl.semaphore_wait(barrier, 11 + extra)

    def remote(src, dst, send, recv, device):
        return pltpu.make_async_remote_copy(
            src_ref=src, dst_ref=dst, send_sem=send, recv_sem=recv, device_id=device, device_id_type=MESH)

    def g_copy(src, i):
        return remote(serp.at[span(i, CD)], gbuf.at[src, span(i, CD)], gs_sem.at[i], gr_sem.at[src, i], (r, 7))

    def x_copy(e, i, row):
        part = xbuf.at[span(i, CD)]
        return remote(part, part, f_sem.at[e, i], x_sem.at[i], (row, c))

    def out_copy(i):
        return remote(obuf.at[i], xbuf.at[span(i, CD)], o_sem.at[i], x_sem.at[i], (out_row, k))

    def via_copy(i):
        return remote(obuf.at[i], abuf.at[0, i], v_sem.at[i], a_sem.at[0, i], (via_row, via_col))

    def hop_copy(i):
        return remote(abuf.at[0, i], xbuf.at[span(i, CD)], v_sem.at[i], x_sem.at[i], (r, via_to))

    def pair_copy(i):
        return remote(obuf.at[i], pin.at[i], o_sem.at[i], p_sem.at[i], (r, c + 1 - 2 * core))

    def sum_copy(s, i):
        return remote(obuf.at[i], abuf.at[s, i], o_sem.at[i], a_sem.at[s, i], (r, sum_col))

    def hand_copy(p, h):
        return remote(zbuf.at[p, h], zin.at[p, h], hs_sem.at[p, h], hr_sem.at[p, h], (r, c + 1 - 2 * core))

    def z_copy(p, h, q):
        return remote(zbuf.at[p, h, q], rbuf.at[chip, p], zs_sem.at[p, h, q], zr_sem.at[chip, p], (r, 4 * h + q))

    def z_wait(src, p):
        remote(zbuf.at[p, 0, 0], rbuf.at[src, p], zs_sem.at[p, 0, 0], zr_sem.at[src, p], (r, 2 * src + 1)).wait_recv()

    def s_copy(d):
        lane = pl.multiple_of((r % 2) * 512 + (d // 2) * 128, 128)
        return remote(xbuf.at[:, pl.ds(lane, 128)], sbuf, ss_sem.at[d], sr_sem, (r, d))

    turned = c == 7
    on_z = jnp.logical_or(turned, dy == 0)
    on_y = jnp.logical_or(jnp.logical_not(turned), dz == 0)
    served = jnp.logical_and(r == root, jnp.logical_or(c == 0, c == 4))
    even = core == 0
    ahead = jnp.logical_or(dz == 0, jnp.logical_and(jnp.logical_not(even), dz == 1))
    behind = jnp.logical_or(dz == 0, jnp.logical_and(even, dz == 3))
    bend = jnp.logical_and(c == 2, r == 14)
    bare = jnp.logical_and(c == 2, r == root)
    edges = (
        (jnp.logical_or(bend, jnp.logical_and(jnp.logical_and(on_z, ahead), jnp.logical_not(served))), zp),
        (jnp.logical_and(on_z, behind), zm),
        (jnp.logical_and(jnp.logical_and(on_y, dy <= 1), jnp.logical_not(bare)), yp),
        (jnp.logical_and(on_y, dy == 0), ym),
    )

    def send_out(i):
        @pl.when(final)
        def _():
            out_copy(i).start()

            @pl.when(via_src)
            def _():
                via_copy(i).start()

        @pl.when(jnp.logical_not(final))
        def _():
            @pl.when(jnp.logical_and(chain, core == 0))
            def _():
                pair_copy(i).start()

            @pl.when(core == 1)
            def _():
                sum_copy(chip, i).start()

    @pl.when(gives)
    def _():
        @pl.loop(0, PAIRS)
        def _(p):
            g_copy(c, 2 * p).start()
            g_copy(c, 2 * p + 1).start()

            @pl.when(r == FIRST)
            def _():
                g_copy(c, 2 * p).wait_send()
                g_copy(c, 2 * p + 1).wait_send()

    slot = step_ref[jnp.maximum(k, 0)] - 2 * r
    shift = r * (COLS * PIECE)

    def pick(first, second):
        return jnp.where(jnp.full(first.shape, slot, jnp.int32) == 0, first, second)

    def pick_rows(ref, j, size):
        return pick(ref[span(j, size), :], ref[pl.ds(pl.multiple_of(BS + j * size, size), size), :])

    def one_hot(row, first):
        pos = lax.broadcasted_iota(jnp.int32, (PIECE, 128), 0) + first
        return jnp.where(pos == row - shift, 1.0, 0.0).astype(BF16)

    @pl.when(uses_d)
    def _():
        @pl.loop(0, 8)
        def _(j):
            load_d(j).wait()

    @pl.when(starts)
    def _():
        @pl.loop(0, 8)
        def _(j):
            hi, lo = split2(pick_rows(df, j, 128).T)
            dhi[:, span(j, 128)] = hi
            dlo[:, span(j, 128)] = lo

    @pl.when(starts)
    def _():
        for q in range(8):
            want = pick(idx_ref[q:q + 1, :], idx_ref[8 + q:9 + q, :])

            @pl.loop(0, COLS)
            def _(s):
                oh[span(s, PIECE), q * 128:(q + 1) * 128] = one_hot(want, s * PIECE)

        @pl.loop(0, PAIRS)
        def _(p):
            hi, lo = split2(serp[span(p, PD), :])
            acc = nn(jnp.concatenate([hi, lo], axis=0), oh[7 * PIECE:, :])
            for s in range(7):
                g_copy(s, 2 * p).wait_recv()
                g_copy(s, 2 * p + 1).wait_recv()
                hi, lo = split2(gbuf[s, span(p, PD), :])
                acc = acc + nn(jnp.concatenate([hi, lo], axis=0), oh[s * PIECE:(s + 1) * PIECE, :])
            both = acc.astype(BF16)
            v = times(both[:PD], both[PD:], dhi[...], dlo[...])
            obuf[2 * p] = v[:CD]
            obuf[2 * p + 1] = v[CD:]
            send_out(2 * p)
            send_out(2 * p + 1)

    @pl.loop(0, 8)
    def _(j):
        load_p(j).wait()

    def turn_panel():
        @pl.loop(0, 8)
        def _(j):
            hi, lo = split2(pf[span(j, PIECE), :].T)
            phi[:, span(j, PIECE)] = hi
            plo[:, span(j, PIECE)] = lo

    @pl.when(chain)
    def _():
        @pl.loop(0, 8)
        def _(j):
            rows = span(j, 128)
            hi, lo = split2(pick_rows(df, j, 128))
            dhi[rows, :] = hi
            dlo[rows, :] = lo
            hi, lo = split2(pick_rows(pf, j, 128))
            oh[rows, :] = hi
            oh[pl.ds(pl.multiple_of(BS + j * 128, 128), 128), :] = lo

        @pl.loop(0, 4)
        def _(j):
            rows = span(j, PIECE)
            th = dhi[rows, :]
            ph = oh[:BS, :]
            m = nn(th, ph) + nn(dlo[rows, :], ph) + nn(th, oh[BS:, :])
            hi, lo = split2(m.T)
            mhi[:, rows] = hi
            mlo[:, rows] = lo

    late_turn = jnp.logical_and(chain, k <= 2)

    @pl.when(jnp.logical_not(late_turn))
    def _():
        turn_panel()

    for q in range(16):
        ohr[q // 2, :, q % 2 * 128:(q % 2 + 1) * 128] = one_hot(idx_ref[q:q + 1, :], c * PIECE)

    def half(p, h):
        hi, lo = split2(xbuf[span(p, PD), :])
        three = jnp.concatenate(split3(serp[span(p, PD), :]), axis=0)

        @pl.when(core == 1)
        def _():
            hand_copy(p, h).wait_recv()

        for q in range(4):
            d = 4 * h + q
            cols = span(d, PIECE)
            a = times(hi, lo, phi[:, cols], plo[:, cols])
            b = nn(three, ohr[d])
            v = b[:PD] + (b[PD:2 * PD] + b[2 * PD:]) - a

            @pl.when(core == 0)
            def _():
                zbuf[p, h, q] = v

            @pl.when(core == 1)
            def _():
                total = v + zin[p, h, q]

                @pl.when(d == c)
                def _():
                    rbuf[chip, p] = total

                @pl.when(d != c)
                def _():
                    zbuf[p, h, q] = total
                    z_copy(p, h, q).start()

        @pl.when(core == 0)
        def _():
            hand_copy(p, h).start()

    def arrive(i):
        x_copy(0, i, zp).wait_recv()

    def forward(i, first=0, last=4):
        for e, (cond, row) in list(enumerate(edges))[first:last]:
            @pl.when(cond)
            def _():
                x_copy(e, i, row).start()

    solves = jnp.logical_and(chain, final)

    @pl.when(via_dev)
    def _():
        @pl.loop(0, CHUNKS)
        def _(i):
            sum_copy(0, i).wait_recv()
            hop_copy(i).start()

    @pl.when(bulk)
    def _():
        @pl.loop(0, CHUNKS)
        def _(i):
            arrive(i)

            forward(i, 0, 2)

            @pl.when(jnp.logical_not(solves))
            def _():
                forward(i, 2, 4)

            @pl.when(chain)
            def _():
                hi, lo = split2(xbuf[span(i, CD), :])
                obuf[i] = times(hi, lo, mhi[...], mlo[...])

                @pl.when(core == 1)
                def _():
                    pair_copy(i).wait_recv()
                    obuf[i] = obuf[i] + pin[i]

                @pl.when(takes)
                def _():
                    sum_copy(chip - 1, i).wait_recv()
                    obuf[i] = obuf[i] + abuf[chip - 1, i]

                @pl.when(final)
                def _():
                    for s in range(CHIPS - 1):
                        @pl.when(jnp.logical_or(s == chip - 1, jnp.logical_and(s == 0, chip == 3)))
                        def _():
                            sum_copy(s, i).wait_recv()
                            obuf[i] = obuf[i] + abuf[s, i]
                    sum_copy(3, i).wait_recv()
                    obuf[i] = abuf[3, i] - obuf[i]

                send_out(i)

            @pl.when(solves)
            def _():
                forward(i, 2, 4)

        @pl.when(late_turn)
        def _():
            turn_panel()

        @pl.loop(0, CHUNKS)
        def _(i):
            half(i // 2, i % 2)

    @pl.when(jnp.logical_not(bulk))
    def _():
        @pl.loop(0, CHUNKS + 2)
        def _(i):
            @pl.when(i < CHUNKS)
            def _():
                arrive(i)
                forward(i)

            @pl.when(i >= 2)
            def _():
                half(i // 2 - 1, i % 2)

    def put_solved(v):
        t = v.T
        sol_ref[...] = jnp.where(jnp.full((64, DATES), core, jnp.int32) == 1, t[64:, :DATES], t[:64, :DATES])

    @pl.when(sol_src)
    def _():
        for d in range(COLS):
            @pl.when(d != c)
            def _():
                s_copy(d).start()
        lane = pl.multiple_of((r % 2) * 512 + chip * 128, 128)
        put_solved(xbuf[:, pl.ds(lane, 128)])

    @pl.when(jnp.logical_not(sol_src))
    def _():
        s_copy(c).wait_recv()
        put_solved(sbuf[...])

    @pl.loop(0, CHIPS)
    def _(s):
        @pl.when(jnp.logical_not(jnp.logical_and(core == 1, s == chip)))
        def _():
            @pl.loop(0, PAIRS)
            def _(p):
                z_wait(s, p)

    total = (rbuf[0] + rbuf[1]) + (rbuf[2] + rbuf[3])
    res_ref[...] = total.reshape(ALL, PIECE)[:DATES, :]

    @pl.loop(0, CHUNKS)
    def _(i):
        @pl.when(jnp.logical_and(gives, r != FIRST))
        def _():
            g_copy(c, i).wait_send()

        for e, (cond, row) in enumerate(edges):
            @pl.when(cond)
            def _():
                x_copy(e, i, row).wait_send()

        @pl.when(uses_d)
        def _():
            pair_copy(i).wait_send()

        @pl.when(jnp.logical_or(via_src, via_dev))
        def _():
            via_copy(i).wait_send()

        @pl.when(core == 0)
        def _():
            hand_copy(i // 2, i % 2).wait_send()

        @pl.when(core == 1)
        def _():
            for q in range(4):
                @pl.when(4 * (i % 2) + q != c)
                def _():
                    z_copy(i // 2, i % 2, q).wait_send()

    @pl.when(sol_src)
    def _():
        for d in range(COLS):
            @pl.when(d != c)
            def _():
                s_copy(d).wait_send()


def body(series, point_order, step_block, panel, diag_inverse):
    idx = point_order.reshape(16, 128)
    vmem = pl.BlockSpec(memory_space=pltpu.VMEM)
    hbm = pl.BlockSpec(memory_space=pl.ANY)
    dma = pltpu.SemaphoreType.DMA
    residual, solved = pl.pallas_call(
        kernel,
        out_shape=(
            jax.ShapeDtypeStruct((DATES, PIECE), F32),
            jax.ShapeDtypeStruct((64, DATES), F32),
        ),
        in_specs=[pl.BlockSpec(memory_space=pltpu.SMEM), vmem, vmem, hbm, hbm],
        out_specs=(vmem, vmem),
        scratch_shapes=[
            pltpu.VMEM((2 * BS, BS), F32),
            pltpu.VMEM((2 * BS, BS), F32),
            pltpu.VMEM((BS, 2 * BS), BF16),
            pltpu.VMEM((BS, 2 * BS), BF16),
            pltpu.VMEM((BS, BS), BF16),
            pltpu.VMEM((BS, BS), BF16),
            pltpu.VMEM((BS, BS), BF16),
            pltpu.VMEM((BS, BS), BF16),
            pltpu.VMEM((2 * BS, BS), BF16),
            pltpu.VMEM((COLS, PIECE, PIECE), BF16),
            pltpu.VMEM((ALL, PIECE), F32),
            pltpu.VMEM((7, ALL, PIECE), F32),
            pltpu.VMEM((ALL, BS), F32),
            pltpu.VMEM((CHUNKS, CD, BS), F32),
            pltpu.VMEM((CHIPS, CHUNKS, CD, BS), F32),
            pltpu.VMEM((CHUNKS, CD, BS), F32),
            pltpu.VMEM((PAIRS, 2, 4, PD, PIECE), F32),
            pltpu.VMEM((PAIRS, 2, 4, PD, PIECE), F32),
            pltpu.VMEM((CHIPS, PAIRS, PD, PIECE), F32),
            pltpu.VMEM((ALL, 128), F32),
            dma((8,)),
            dma((8,)),
            dma((CHUNKS,)),
            dma((7, CHUNKS)),
            dma((4, CHUNKS)),
            dma((CHUNKS,)),
            dma((CHUNKS,)),
            dma((CHUNKS,)),
            dma((CHUNKS,)),
            dma((CHIPS, CHUNKS)),
            dma((PAIRS, 2, 4)),
            dma((CHIPS, PAIRS)),
            dma((PAIRS, 2)),
            dma((PAIRS, 2)),
            dma((COLS,)),
            dma,
        ],
        compiler_params=pltpu.CompilerParams(
            collective_id=0, has_side_effects=True, vmem_limit_bytes=60 * 1024 * 1024
        ),
    )(step_block, idx, series, panel, diag_inverse)
    return solved, residual.T


def solution(mesh):
    in_specs = (P(None, ("rows", "cols")), P("rows"), P(), P("rows", "cols"), P("rows", None))
    out_specs = (P(("rows", "cols"), None), P(("rows", "cols"), None))
    return jax.shard_map(body, mesh=mesh, in_specs=in_specs, out_specs=out_specs, check_vma=False)
```

```python
import jax
import jax.numpy as jnp
from jax import lax
from jax.experimental import pallas as pl
from jax.experimental.pallas import tpu as pltpu
from jax.sharding import PartitionSpec as P

MESH = pl.DeviceIdType.MESH
F32 = jnp.float32
BF16 = jnp.bfloat16
DATES = 300
CHUNKS = 10
CD = 32
LAST = 16
PAIRS = CHUNKS // 2
PD = 2 * CD
ALL = CHUNKS * CD
BS = 1024
COLS = 8
CHIPS = 4
PIECE = 256
FIRST = 8


def split2(v):
    hi = v.astype(BF16)
    return hi, (v - hi.astype(F32)).astype(BF16)


def split3(v):
    hi = v.astype(BF16)
    rest = v - hi.astype(F32)
    mid = rest.astype(BF16)
    return hi, mid, (rest - mid.astype(F32)).astype(BF16)


def nn(a, b):
    return lax.dot_general(a, b, (((1,), (0,)), ((), ())), preferred_element_type=F32)


def times(hi, lo, weight_hi, weight_lo):
    n = hi.shape[0]
    a = nn(jnp.concatenate([hi, lo], axis=0), weight_hi)
    return a[:n] + (a[n:] + nn(hi, weight_lo))


def span(j, size):
    return pl.ds(pl.multiple_of(j * size, size), size)


def kernel(step_ref, idx_ref, ser_ref, panel_ref, diag_ref, res_ref, sol_ref,
           pf, df, phi, plo, mhi, mlo, dhi, dlo, oh, ohr, serp, gbuf, xbuf, pin, abuf, obuf, zbuf, zin, rbuf, sbuf,
           pl_sem, dl_sem, gs_sem, gr_sem, f_sem, x_sem, o_sem, v_sem, p_sem, a_sem, zs_sem, zr_sem, hs_sem, hr_sem, ss_sem, sr_sem):
    r = lax.axis_index("rows")
    c = lax.axis_index("cols")
    k = r - FIRST
    y, z = r // 4, r % 4
    chip, core = c // 2, c % 2
    root = FIRST + 1 + jnp.minimum(c, 6)
    dy = (y - root // 4 + 4) % 4
    dz = (z - root % 4 + 4) % 4
    late = r >= FIRST
    chain = jnp.logical_and(late, c < k)
    starts = jnp.logical_and(late, c == 7)
    gives = jnp.logical_and(late, c < 7)
    uses_d = jnp.logical_or(chain, starts)
    bulk = jnp.logical_and(jnp.logical_and(late, 2 * chip < k), jnp.logical_not(jnp.logical_and(r == 15, c == 7)))
    final = jnp.logical_and(late, c == (k + 15) % 8)
    diag_src = jnp.logical_and(final, r < 15)
    diag_dst = jnp.logical_and(c < 7, r == root)
    solver = jnp.maximum(k - 1, 0)
    solver_chip = solver // 2
    near = jnp.logical_or(chip + 1 == solver_chip, jnp.logical_or(c == 7, jnp.logical_and(chip == 0, solver_chip == 3)))
    sum_col = jnp.where(near, solver, jnp.minimum(c + 2, 7))
    takes = jnp.logical_and(jnp.logical_and(chain, core == 1), jnp.logical_and(chip >= 1, chip + 1 == solver_chip))
    via_src = jnp.logical_or(jnp.logical_and(r == 8, c == 7), jnp.logical_and(r == 12, c == 3))
    via_dev = jnp.logical_or(jnp.logical_and(r == 10, c == 6), jnp.logical_and(r == 14, c == 7))
    via_row = jnp.minimum(r + 2, 15)
    via_col = jnp.where(r == 8, 6, 7)
    via_from = jnp.where(r == 10, 7, 3)
    via_to = jnp.where(r == 10, 0, 4)
    out_row = jnp.minimum(r + 1, 15)
    prev_col = (c + 7) % 8
    sol_src = c == r // 2

    zp, zm = y * 4 + (z + 1) % 4, y * 4 + (z + 3) % 4
    yp, ym = ((y + 1) % 4) * 4 + z, ((y + 3) % 4) * 4 + z

    barrier = pltpu.get_barrier_semaphore()
    for other in (zp, zm, yp, ym):
        pl.semaphore_signal(barrier, inc=1, device_id=(other, c), device_id_type=MESH)
    for d in range(1, COLS):
        pl.semaphore_signal(barrier, inc=1, device_id=(r, (c + d) % COLS), device_id_type=MESH)

    @pl.when(diag_src)
    def _():
        pl.semaphore_signal(barrier, inc=1, device_id=(out_row, k), device_id_type=MESH)

    @pl.when(diag_dst)
    def _():
        pl.semaphore_signal(barrier, inc=1, device_id=(r - 1, prev_col), device_id_type=MESH)

    @pl.when(via_src)
    def _():
        pl.semaphore_signal(barrier, inc=1, device_id=(via_row, via_col), device_id_type=MESH)

    @pl.when(via_dev)
    def _():
        pl.semaphore_signal(barrier, inc=1, device_id=(jnp.maximum(r - 2, 0), via_from), device_id_type=MESH)

    def load_d(j):
        rows = span(j, PIECE)
        return pltpu.make_async_copy(diag_ref.at[rows], df.at[rows], dl_sem.at[j])

    def load_p(j):
        rows = span(j, PIECE)
        return pltpu.make_async_copy(panel_ref.at[rows], pf.at[rows], pl_sem.at[j])

    @pl.when(uses_d)
    def _():
        for j in range(8):
            load_d(j).start()

    for j in range(8):
        load_p(j).start()

    whole = DATES // CD * CD
    serp[:whole, :] = ser_ref[:whole, :]
    serp[whole:, :] = jnp.concatenate(
        [ser_ref[whole:, :], jnp.zeros((ALL - DATES, PIECE), F32)], axis=0)

    xbuf[ALL - LAST:, :] = jnp.zeros((LAST, BS), F32)
    one = jnp.int32(1)
    zero = jnp.int32(0)
    extra = sum(jnp.where(cond, one, zero) for cond in (diag_src, diag_dst, via_src, via_dev))
    pl.semaphore_wait(barrier, 11 + extra)

    class Sized:
        def __init__(self, make, i):
            self.make, self.i = make, i

        def each(self, act):
            @pl.when(self.i < CHUNKS - 1)
            def _():
                act(self.make(CD))

            @pl.when(self.i == CHUNKS - 1)
            def _():
                act(self.make(LAST))

        def start(self):
            self.each(lambda copy: copy.start())

        def wait_send(self):
            self.each(lambda copy: copy.wait_send())

        def wait_recv(self):
            self.each(lambda copy: copy.wait_recv())

    def rows_of(i, n):
        return pl.ds(pl.multiple_of(i * CD, CD), n)

    def remote(src, dst, send, recv, device):
        return pltpu.make_async_remote_copy(
            src_ref=src, dst_ref=dst, send_sem=send, recv_sem=recv, device_id=device, device_id_type=MESH)

    def g_copy(src, i):
        return remote(serp.at[span(i, CD)], gbuf.at[src, span(i, CD)], gs_sem.at[i], gr_sem.at[src, i], (r, 7))

    def x_copy(e, i, row):
        def make(n):
            part = xbuf.at[rows_of(i, n)]
            return remote(part, part, f_sem.at[e, i], x_sem.at[i], (row, c))
        return Sized(make, i)

    def out_copy(i):
        return Sized(lambda n: remote(
            obuf.at[i, pl.ds(0, n)], xbuf.at[rows_of(i, n)], o_sem.at[i], x_sem.at[i], (out_row, k)), i)

    def via_copy(i):
        return Sized(lambda n: remote(
            obuf.at[i, pl.ds(0, n)], abuf.at[0, i, pl.ds(0, n)], v_sem.at[i], a_sem.at[0, i], (via_row, via_col)), i)

    def hop_copy(i):
        return Sized(lambda n: remote(
            abuf.at[0, i, pl.ds(0, n)], xbuf.at[rows_of(i, n)], v_sem.at[i], x_sem.at[i], (r, via_to)), i)

    def pair_copy(i):
        return Sized(lambda n: remote(
            obuf.at[i, pl.ds(0, n)], pin.at[i, pl.ds(0, n)], o_sem.at[i], p_sem.at[i], (r, c + 1 - 2 * core)), i)

    def sum_copy(s, i):
        return Sized(lambda n: remote(
            obuf.at[i, pl.ds(0, n)], abuf.at[s, i, pl.ds(0, n)], o_sem.at[i], a_sem.at[s, i], (r, sum_col)), i)

    def hand_copy(p, h):
        return remote(zbuf.at[p, h], zin.at[p, h], hs_sem.at[p, h], hr_sem.at[p, h], (r, c + 1 - 2 * core))

    def z_copy(p, h, q):
        return remote(zbuf.at[p, h, q], rbuf.at[chip, p], zs_sem.at[p, h, q], zr_sem.at[chip, p], (r, 4 * h + q))

    def z_wait(src, p):
        remote(zbuf.at[p, 0, 0], rbuf.at[src, p], zs_sem.at[p, 0, 0], zr_sem.at[src, p], (r, 2 * src + 1)).wait_recv()

    def s_copy(d):
        lane = pl.multiple_of((r % 2) * 512 + (d // 2) * 128, 128)
        return remote(xbuf.at[:, pl.ds(lane, 128)], sbuf, ss_sem.at[d], sr_sem, (r, d))

    turned = c == 7
    on_z = jnp.logical_or(turned, dy == 0)
    on_y = jnp.logical_or(jnp.logical_not(turned), dz == 0)
    served = jnp.logical_and(r == root, jnp.logical_or(c == 0, c == 4))
    even = core == 0
    ahead = jnp.logical_or(dz == 0, jnp.logical_and(jnp.logical_not(even), dz == 1))
    behind = jnp.logical_or(dz == 0, jnp.logical_and(even, dz == 3))
    bend = jnp.logical_and(c == 2, r == 14)
    bare = jnp.logical_and(c == 2, r == root)
    edges = (
        (jnp.logical_or(bend, jnp.logical_and(jnp.logical_and(on_z, ahead), jnp.logical_not(served))), zp),
        (jnp.logical_and(on_z, behind), zm),
        (jnp.logical_and(jnp.logical_and(on_y, dy <= 1), jnp.logical_not(bare)), yp),
        (jnp.logical_and(on_y, dy == 0), ym),
    )

    def send_out(i):
        @pl.when(final)
        def _():
            out_copy(i).start()

            @pl.when(via_src)
            def _():
                via_copy(i).start()

        @pl.when(jnp.logical_not(final))
        def _():
            @pl.when(jnp.logical_and(chain, core == 0))
            def _():
                pair_copy(i).start()

            @pl.when(core == 1)
            def _():
                sum_copy(chip, i).start()

    @pl.when(gives)
    def _():
        @pl.loop(0, PAIRS)
        def _(p):
            g_copy(c, 2 * p).start()
            g_copy(c, 2 * p + 1).start()

            @pl.when(r == FIRST)
            def _():
                g_copy(c, 2 * p).wait_send()
                g_copy(c, 2 * p + 1).wait_send()

    slot = step_ref[jnp.maximum(k, 0)] - 2 * r
    shift = r * (COLS * PIECE)

    def pick(first, second):
        return jnp.where(jnp.full(first.shape, slot, jnp.int32) == 0, first, second)

    def pick_rows(ref, j, size):
        return pick(ref[span(j, size), :], ref[pl.ds(pl.multiple_of(BS + j * size, size), size), :])

    def one_hot(row, first):
        pos = lax.broadcasted_iota(jnp.int32, (PIECE, 128), 0) + first
        return jnp.where(pos == row - shift, 1.0, 0.0).astype(BF16)

    @pl.when(uses_d)
    def _():
        @pl.loop(0, 8)
        def _(j):
            load_d(j).wait()

    @pl.when(starts)
    def _():
        @pl.loop(0, 8)
        def _(j):
            hi, lo = split2(pick_rows(df, j, 128).T)
            dhi[:, span(j, 128)] = hi
            dlo[:, span(j, 128)] = lo

    @pl.when(starts)
    def _():
        for q in range(8):
            want = pick(idx_ref[q:q + 1, :], idx_ref[8 + q:9 + q, :])

            @pl.loop(0, COLS)
            def _(s):
                oh[span(s, PIECE), q * 128:(q + 1) * 128] = one_hot(want, s * PIECE)

        @pl.loop(0, PAIRS)
        def _(p):
            hi, lo = split2(serp[span(p, PD), :])
            acc = nn(jnp.concatenate([hi, lo], axis=0), oh[7 * PIECE:, :])
            for s in range(7):
                g_copy(s, 2 * p).wait_recv()
                g_copy(s, 2 * p + 1).wait_recv()
                hi, lo = split2(gbuf[s, span(p, PD), :])
                acc = acc + nn(jnp.concatenate([hi, lo], axis=0), oh[s * PIECE:(s + 1) * PIECE, :])
            both = acc.astype(BF16)
            v = times(both[:PD], both[PD:], dhi[...], dlo[...])
            obuf[2 * p] = v[:CD]
            obuf[2 * p + 1] = v[CD:]
            send_out(2 * p)
            send_out(2 * p + 1)

    @pl.loop(0, 8)
    def _(j):
        load_p(j).wait()

    def turn_panel():
        @pl.loop(0, 8)
        def _(j):
            hi, lo = split2(pf[span(j, PIECE), :].T)
            phi[:, span(j, PIECE)] = hi
            plo[:, span(j, PIECE)] = lo

    @pl.when(chain)
    def _():
        @pl.loop(0, 8)
        def _(j):
            rows = span(j, 128)
            hi, lo = split2(pick_rows(df, j, 128))
            dhi[rows, :] = hi
            dlo[rows, :] = lo
            hi, lo = split2(pick_rows(pf, j, 128))
            oh[rows, :] = hi
            oh[pl.ds(pl.multiple_of(BS + j * 128, 128), 128), :] = lo

        @pl.loop(0, 4)
        def _(j):
            rows = span(j, PIECE)
            th = dhi[rows, :]
            ph = oh[:BS, :]
            m = nn(th, ph) + nn(dlo[rows, :], ph) + nn(th, oh[BS:, :])
            hi, lo = split2(m.T)
            mhi[:, rows] = hi
            mlo[:, rows] = lo

    late_turn = jnp.logical_and(chain, k <= 2)

    @pl.when(jnp.logical_not(late_turn))
    def _():
        turn_panel()

    for q in range(16):
        ohr[q // 2, :, q % 2 * 128:(q % 2 + 1) * 128] = one_hot(idx_ref[q:q + 1, :], c * PIECE)

    def half(p, h):
        hi, lo = split2(xbuf[span(p, PD), :])
        three = jnp.concatenate(split3(serp[span(p, PD), :]), axis=0)

        @pl.when(core == 1)
        def _():
            hand_copy(p, h).wait_recv()

        for q in range(4):
            d = 4 * h + q
            cols = span(d, PIECE)
            a = times(hi, lo, phi[:, cols], plo[:, cols])
            b = nn(three, ohr[d])
            v = b[:PD] + (b[PD:2 * PD] + b[2 * PD:]) - a

            @pl.when(core == 0)
            def _():
                zbuf[p, h, q] = v

            @pl.when(core == 1)
            def _():
                total = v + zin[p, h, q]

                @pl.when(d == c)
                def _():
                    rbuf[chip, p] = total

                @pl.when(d != c)
                def _():
                    zbuf[p, h, q] = total
                    z_copy(p, h, q).start()

        @pl.when(core == 0)
        def _():
            hand_copy(p, h).start()

    def arrive(i):
        x_copy(0, i, zp).wait_recv()

    def forward(i, first=0, last=4):
        for e, (cond, row) in list(enumerate(edges))[first:last]:
            @pl.when(cond)
            def _():
                x_copy(e, i, row).start()

    solves = jnp.logical_and(chain, final)
    early = jnp.logical_and(r == 15, c == 6)

    @pl.when(via_dev)
    def _():
        @pl.loop(0, CHUNKS)
        def _(i):
            sum_copy(0, i).wait_recv()
            hop_copy(i).start()

    @pl.when(bulk)
    def _():
        @pl.loop(0, CHUNKS)
        def _(i):
            arrive(i)

            forward(i, 0, 2)

            @pl.when(jnp.logical_not(solves))
            def _():
                forward(i, 2, 4)

            @pl.when(chain)
            def _():
                hi, lo = split2(xbuf[span(i, CD), :])
                obuf[i] = times(hi, lo, mhi[...], mlo[...])

                @pl.when(core == 1)
                def _():
                    pair_copy(i).wait_recv()
                    obuf[i] = obuf[i] + pin[i]

                @pl.when(takes)
                def _():
                    sum_copy(chip - 1, i).wait_recv()
                    obuf[i] = obuf[i] + abuf[chip - 1, i]

                @pl.when(final)
                def _():
                    for s in range(CHIPS - 1):
                        @pl.when(jnp.logical_or(s == chip - 1, jnp.logical_and(s == 0, chip == 3)))
                        def _():
                            sum_copy(s, i).wait_recv()
                            obuf[i] = obuf[i] + abuf[s, i]
                    sum_copy(3, i).wait_recv()
                    obuf[i] = abuf[3, i] - obuf[i]

                send_out(i)

            @pl.when(solves)
            def _():
                forward(i, 2, 4)

            @pl.when(jnp.logical_and(early, i >= 2))
            def _():
                half(i // 2 - 1, i % 2)

        @pl.when(late_turn)
        def _():
            turn_panel()

        @pl.loop(jnp.where(early, CHUNKS - 2, 0), CHUNKS)
        def _(i):
            half(i // 2, i % 2)

    @pl.when(jnp.logical_not(bulk))
    def _():
        @pl.loop(0, CHUNKS + 2)
        def _(i):
            @pl.when(i < CHUNKS)
            def _():
                arrive(i)
                forward(i)

            @pl.when(i >= 2)
            def _():
                half(i // 2 - 1, i % 2)

    def put_solved(v):
        t = v.T
        sol_ref[...] = jnp.where(jnp.full((64, DATES), core, jnp.int32) == 1, t[64:, :DATES], t[:64, :DATES])

    @pl.when(sol_src)
    def _():
        for d in range(COLS):
            @pl.when(d != c)
            def _():
                s_copy(d).start()
        lane = pl.multiple_of((r % 2) * 512 + chip * 128, 128)
        put_solved(xbuf[:, pl.ds(lane, 128)])

    @pl.when(jnp.logical_not(sol_src))
    def _():
        s_copy(c).wait_recv()
        put_solved(sbuf[...])

    @pl.loop(0, CHIPS)
    def _(s):
        @pl.when(jnp.logical_not(jnp.logical_and(core == 1, s == chip)))
        def _():
            @pl.loop(0, PAIRS)
            def _(p):
                z_wait(s, p)

    total = (rbuf[0] + rbuf[1]) + (rbuf[2] + rbuf[3])
    res_ref[...] = total.reshape(ALL, PIECE)[:DATES, :]

    @pl.loop(0, CHUNKS)
    def _(i):
        @pl.when(jnp.logical_and(gives, r != FIRST))
        def _():
            g_copy(c, i).wait_send()

        for e, (cond, row) in enumerate(edges):
            @pl.when(cond)
            def _():
                x_copy(e, i, row).wait_send()

        @pl.when(uses_d)
        def _():
            pair_copy(i).wait_send()

        @pl.when(jnp.logical_or(via_src, via_dev))
        def _():
            via_copy(i).wait_send()

        @pl.when(core == 0)
        def _():
            hand_copy(i // 2, i % 2).wait_send()

        @pl.when(core == 1)
        def _():
            for q in range(4):
                @pl.when(4 * (i % 2) + q != c)
                def _():
                    z_copy(i // 2, i % 2, q).wait_send()

    @pl.when(sol_src)
    def _():
        for d in range(COLS):
            @pl.when(d != c)
            def _():
                s_copy(d).wait_send()


def body(series, point_order, step_block, panel, diag_inverse):
    idx = point_order.reshape(16, 128)
    vmem = pl.BlockSpec(memory_space=pltpu.VMEM)
    hbm = pl.BlockSpec(memory_space=pl.ANY)
    dma = pltpu.SemaphoreType.DMA
    residual, solved = pl.pallas_call(
        kernel,
        out_shape=(
            jax.ShapeDtypeStruct((DATES, PIECE), F32),
            jax.ShapeDtypeStruct((64, DATES), F32),
        ),
        in_specs=[pl.BlockSpec(memory_space=pltpu.SMEM), vmem, vmem, hbm, hbm],
        out_specs=(vmem, vmem),
        scratch_shapes=[
            pltpu.VMEM((2 * BS, BS), F32),
            pltpu.VMEM((2 * BS, BS), F32),
            pltpu.VMEM((BS, 2 * BS), BF16),
            pltpu.VMEM((BS, 2 * BS), BF16),
            pltpu.VMEM((BS, BS), BF16),
            pltpu.VMEM((BS, BS), BF16),
            pltpu.VMEM((BS, BS), BF16),
            pltpu.VMEM((BS, BS), BF16),
            pltpu.VMEM((2 * BS, BS), BF16),
            pltpu.VMEM((COLS, PIECE, PIECE), BF16),
            pltpu.VMEM((ALL, PIECE), F32),
            pltpu.VMEM((7, ALL, PIECE), F32),
            pltpu.VMEM((ALL, BS), F32),
            pltpu.VMEM((CHUNKS, CD, BS), F32),
            pltpu.VMEM((CHIPS, CHUNKS, CD, BS), F32),
            pltpu.VMEM((CHUNKS, CD, BS), F32),
            pltpu.VMEM((PAIRS, 2, 4, PD, PIECE), F32),
            pltpu.VMEM((PAIRS, 2, 4, PD, PIECE), F32),
            pltpu.VMEM((CHIPS, PAIRS, PD, PIECE), F32),
            pltpu.VMEM((ALL, 128), F32),
            dma((8,)),
            dma((8,)),
            dma((CHUNKS,)),
            dma((7, CHUNKS)),
            dma((4, CHUNKS)),
            dma((CHUNKS,)),
            dma((CHUNKS,)),
            dma((CHUNKS,)),
            dma((CHUNKS,)),
            dma((CHIPS, CHUNKS)),
            dma((PAIRS, 2, 4)),
            dma((CHIPS, PAIRS)),
            dma((PAIRS, 2)),
            dma((PAIRS, 2)),
            dma((COLS,)),
            dma,
        ],
        compiler_params=pltpu.CompilerParams(
            collective_id=0, has_side_effects=True, vmem_limit_bytes=60 * 1024 * 1024
        ),
    )(step_block, idx, series, panel, diag_inverse)
    return solved, residual.T


def solution(mesh):
    in_specs = (P(None, ("rows", "cols")), P("rows"), P(), P("rows", "cols"), P("rows", None))
    out_specs = (P(("rows", "cols"), None), P(("rows", "cols"), None))
    return jax.shard_map(body, mesh=mesh, in_specs=in_specs, out_specs=out_specs, check_vma=False)
```

```python
import jax
import jax.numpy as jnp
from jax import lax
from jax.experimental import pallas as pl
from jax.experimental.pallas import tpu as pltpu
from jax.sharding import PartitionSpec as P

MESH = pl.DeviceIdType.MESH
F32 = jnp.float32
BF16 = jnp.bfloat16
DATES = 300
CHUNKS = 10
CD = 32
LAST = 16
PAIRS = CHUNKS // 2
PD = 2 * CD
ALL = CHUNKS * CD
BS = 1024
COLS = 8
CHIPS = 4
PIECE = 256
FIRST = 8


def split2(v):
    hi = v.astype(BF16)
    return hi, (v - hi.astype(F32)).astype(BF16)


def split3(v):
    hi = v.astype(BF16)
    rest = v - hi.astype(F32)
    mid = rest.astype(BF16)
    return hi, mid, (rest - mid.astype(F32)).astype(BF16)


def nn(a, b):
    return lax.dot_general(a, b, (((1,), (0,)), ((), ())), preferred_element_type=F32)


def times(hi, lo, weight_hi, weight_lo):
    n = hi.shape[0]
    a = nn(jnp.concatenate([hi, lo], axis=0), weight_hi)
    return a[:n] + (a[n:] + nn(hi, weight_lo))


def span(j, size):
    return pl.ds(pl.multiple_of(j * size, size), size)


def kernel(step_ref, idx_ref, ser_ref, panel_ref, diag_ref, res_ref, sol_ref,
           pf, df, phi, plo, mhi, mlo, dhi, dlo, oh, ohr, serp, gbuf, xbuf, pin, abuf, obuf, zbuf, zin, rbuf, sbuf,
           pl_sem, dl_sem, gs_sem, gr_sem, f_sem, x_sem, o_sem, v_sem, p_sem, a_sem, zs_sem, zr_sem, hs_sem, hr_sem, ss_sem, sr_sem):
    r = lax.axis_index("rows")
    c = lax.axis_index("cols")
    k = r - FIRST
    y, z = r // 4, r % 4
    chip, core = c // 2, c % 2
    root = FIRST + 1 + jnp.minimum(c, 6)
    dy = (y - root // 4 + 4) % 4
    dz = (z - root % 4 + 4) % 4
    late = r >= FIRST
    chain = jnp.logical_and(late, c < k)
    starts = jnp.logical_and(late, c == 7)
    gives = jnp.logical_and(late, c < 7)
    uses_d = jnp.logical_or(chain, starts)
    bulk = jnp.logical_and(jnp.logical_and(late, 2 * chip < k), jnp.logical_not(jnp.logical_and(r == 15, c == 7)))
    final = jnp.logical_and(late, c == (k + 15) % 8)
    diag_src = jnp.logical_and(final, r < 15)
    diag_dst = jnp.logical_and(c < 7, r == root)
    solver = jnp.maximum(k - 1, 0)
    solver_chip = solver // 2
    near = jnp.logical_or(chip + 1 == solver_chip, jnp.logical_or(c == 7, jnp.logical_and(chip == 0, solver_chip == 3)))
    sum_col = jnp.where(near, solver, jnp.minimum(c + 2, 7))
    takes = jnp.logical_and(jnp.logical_and(chain, core == 1), jnp.logical_and(chip >= 1, chip + 1 == solver_chip))
    via_src = jnp.logical_or(jnp.logical_and(r == 8, c == 7), jnp.logical_and(r == 12, c == 3))
    via_dev = jnp.logical_or(jnp.logical_and(r == 10, c == 6), jnp.logical_and(r == 14, c == 7))
    via_row = jnp.minimum(r + 2, 15)
    via_col = jnp.where(r == 8, 6, 7)
    via_from = jnp.where(r == 10, 7, 3)
    via_to = jnp.where(r == 10, 0, 4)
    out_row = jnp.minimum(r + 1, 15)
    prev_col = (c + 7) % 8
    sol_src = c == r // 2

    zp, zm = y * 4 + (z + 1) % 4, y * 4 + (z + 3) % 4
    yp, ym = ((y + 1) % 4) * 4 + z, ((y + 3) % 4) * 4 + z

    barrier = pltpu.get_barrier_semaphore()
    for other in (zp, zm, yp, ym):
        pl.semaphore_signal(barrier, inc=1, device_id=(other, c), device_id_type=MESH)
    for d in range(1, COLS):
        pl.semaphore_signal(barrier, inc=1, device_id=(r, (c + d) % COLS), device_id_type=MESH)

    @pl.when(diag_src)
    def _():
        pl.semaphore_signal(barrier, inc=1, device_id=(out_row, k), device_id_type=MESH)

    @pl.when(diag_dst)
    def _():
        pl.semaphore_signal(barrier, inc=1, device_id=(r - 1, prev_col), device_id_type=MESH)

    @pl.when(via_src)
    def _():
        pl.semaphore_signal(barrier, inc=1, device_id=(via_row, via_col), device_id_type=MESH)

    @pl.when(via_dev)
    def _():
        pl.semaphore_signal(barrier, inc=1, device_id=(jnp.maximum(r - 2, 0), via_from), device_id_type=MESH)

    def load_d(j):
        rows = span(j, PIECE)
        return pltpu.make_async_copy(diag_ref.at[rows], df.at[rows], dl_sem.at[j])

    def load_p(j):
        rows = span(j, PIECE)
        return pltpu.make_async_copy(panel_ref.at[rows], pf.at[rows], pl_sem.at[j])

    @pl.when(uses_d)
    def _():
        for j in range(8):
            load_d(j).start()

    for j in range(8):
        load_p(j).start()

    whole = DATES // CD * CD
    serp[:whole, :] = ser_ref[:whole, :]
    serp[whole:, :] = jnp.concatenate(
        [ser_ref[whole:, :], jnp.zeros((ALL - DATES, PIECE), F32)], axis=0)

    xbuf[ALL - LAST:, :] = jnp.zeros((LAST, BS), F32)
    one = jnp.int32(1)
    zero = jnp.int32(0)
    extra = sum(jnp.where(cond, one, zero) for cond in (diag_src, diag_dst, via_src, via_dev))
    pl.semaphore_wait(barrier, 11 + extra)

    class Sized:
        def __init__(self, make, i):
            self.make, self.i = make, i

        def each(self, act):
            @pl.when(self.i < CHUNKS - 1)
            def _():
                act(self.make(CD))

            @pl.when(self.i == CHUNKS - 1)
            def _():
                act(self.make(LAST))

        def start(self):
            self.each(lambda copy: copy.start())

        def wait_send(self):
            self.each(lambda copy: copy.wait_send())

        def wait_recv(self):
            self.each(lambda copy: copy.wait_recv())

    def rows_of(i, n):
        return pl.ds(pl.multiple_of(i * CD, CD), n)

    def remote(src, dst, send, recv, device):
        return pltpu.make_async_remote_copy(
            src_ref=src, dst_ref=dst, send_sem=send, recv_sem=recv, device_id=device, device_id_type=MESH)

    def g_copy(src, i):
        return remote(serp.at[span(i, CD)], gbuf.at[src, span(i, CD)], gs_sem.at[i], gr_sem.at[src, i], (r, 7))

    def x_copy(e, i, row):
        def make(n):
            part = xbuf.at[rows_of(i, n)]
            return remote(part, part, f_sem.at[e, i], x_sem.at[i], (row, c))
        return Sized(make, i)

    def out_copy(i):
        return Sized(lambda n: remote(
            obuf.at[i, pl.ds(0, n)], xbuf.at[rows_of(i, n)], o_sem.at[i], x_sem.at[i], (out_row, k)), i)

    def via_copy(i):
        return Sized(lambda n: remote(
            obuf.at[i, pl.ds(0, n)], abuf.at[0, i, pl.ds(0, n)], v_sem.at[i], a_sem.at[0, i], (via_row, via_col)), i)

    def hop_copy(i):
        return Sized(lambda n: remote(
            abuf.at[0, i, pl.ds(0, n)], xbuf.at[rows_of(i, n)], v_sem.at[i], x_sem.at[i], (r, via_to)), i)

    def pair_copy(i):
        return Sized(lambda n: remote(
            obuf.at[i, pl.ds(0, n)], pin.at[i, pl.ds(0, n)], o_sem.at[i], p_sem.at[i], (r, c + 1 - 2 * core)), i)

    def sum_copy(s, i):
        return Sized(lambda n: remote(
            obuf.at[i, pl.ds(0, n)], abuf.at[s, i, pl.ds(0, n)], o_sem.at[i], a_sem.at[s, i], (r, sum_col)), i)

    def hand_copy(p, h):
        return remote(zbuf.at[p, h], zin.at[p, h], hs_sem.at[p, h], hr_sem.at[p, h], (r, c + 1 - 2 * core))

    def z_copy(p, h, q):
        return remote(zbuf.at[p, h, q], rbuf.at[chip, p], zs_sem.at[p, h, q], zr_sem.at[chip, p], (r, 4 * h + q))

    def z_wait(src, p):
        remote(zbuf.at[p, 0, 0], rbuf.at[src, p], zs_sem.at[p, 0, 0], zr_sem.at[src, p], (r, 2 * src + 1)).wait_recv()

    def s_copy(d):
        lane = pl.multiple_of((r % 2) * 512 + (d // 2) * 128, 128)
        return remote(xbuf.at[:, pl.ds(lane, 128)], sbuf, ss_sem.at[d], sr_sem, (r, d))

    turned = c == 7
    on_z = jnp.logical_or(turned, dy == 0)
    on_y = jnp.logical_or(jnp.logical_not(turned), dz == 0)
    served = jnp.logical_and(r == root, jnp.logical_or(c == 0, c == 4))
    even = core == 0
    ahead = jnp.logical_or(dz == 0, jnp.logical_and(jnp.logical_not(even), dz == 1))
    behind = jnp.logical_or(dz == 0, jnp.logical_and(even, dz == 3))
    bend = jnp.logical_and(c == 2, r == 14)
    bare = jnp.logical_and(c == 2, r == root)
    edges = (
        (jnp.logical_or(bend, jnp.logical_and(jnp.logical_and(on_z, ahead), jnp.logical_not(served))), zp),
        (jnp.logical_and(on_z, behind), zm),
        (jnp.logical_and(jnp.logical_and(on_y, dy <= 1), jnp.logical_not(bare)), yp),
        (jnp.logical_and(on_y, dy == 0), ym),
    )

    def send_out(i):
        @pl.when(final)
        def _():
            out_copy(i).start()

            @pl.when(via_src)
            def _():
                via_copy(i).start()

        @pl.when(jnp.logical_not(final))
        def _():
            @pl.when(jnp.logical_and(chain, core == 0))
            def _():
                pair_copy(i).start()

            @pl.when(core == 1)
            def _():
                sum_copy(chip, i).start()

    @pl.when(gives)
    def _():
        @pl.loop(0, PAIRS)
        def _(p):
            g_copy(c, 2 * p).start()
            g_copy(c, 2 * p + 1).start()

            @pl.when(jnp.logical_or(r == FIRST, jnp.logical_not(chain)))
            def _():
                g_copy(c, 2 * p).wait_send()
                g_copy(c, 2 * p + 1).wait_send()

    slot = step_ref[jnp.maximum(k, 0)] - 2 * r
    shift = r * (COLS * PIECE)

    def pick(first, second):
        return jnp.where(jnp.full(first.shape, slot, jnp.int32) == 0, first, second)

    def pick_rows(ref, j, size):
        return pick(ref[span(j, size), :], ref[pl.ds(pl.multiple_of(BS + j * size, size), size), :])

    def one_hot(row, first):
        pos = lax.broadcasted_iota(jnp.int32, (PIECE, 128), 0) + first
        return jnp.where(pos == row - shift, 1.0, 0.0).astype(BF16)

    @pl.when(uses_d)
    def _():
        @pl.loop(0, 8)
        def _(j):
            load_d(j).wait()

    @pl.when(starts)
    def _():
        @pl.loop(0, 8)
        def _(j):
            hi, lo = split2(pick_rows(df, j, 128).T)
            dhi[:, span(j, 128)] = hi
            dlo[:, span(j, 128)] = lo

    @pl.when(starts)
    def _():
        for q in range(8):
            want = pick(idx_ref[q:q + 1, :], idx_ref[8 + q:9 + q, :])

            @pl.loop(0, COLS)
            def _(s):
                oh[span(s, PIECE), q * 128:(q + 1) * 128] = one_hot(want, s * PIECE)

        @pl.loop(0, PAIRS)
        def _(p):
            hi, lo = split2(serp[span(p, PD), :])
            acc = nn(jnp.concatenate([hi, lo], axis=0), oh[7 * PIECE:, :])
            for s in range(7):
                g_copy(s, 2 * p).wait_recv()
                g_copy(s, 2 * p + 1).wait_recv()
                hi, lo = split2(gbuf[s, span(p, PD), :])
                acc = acc + nn(jnp.concatenate([hi, lo], axis=0), oh[s * PIECE:(s + 1) * PIECE, :])
            both = acc.astype(BF16)
            v = times(both[:PD], both[PD:], dhi[...], dlo[...])
            obuf[2 * p] = v[:CD]
            obuf[2 * p + 1] = v[CD:]
            send_out(2 * p)
            send_out(2 * p + 1)

    @pl.loop(0, 8)
    def _(j):
        load_p(j).wait()

    def turn_panel():
        @pl.loop(0, 8)
        def _(j):
            hi, lo = split2(pf[span(j, PIECE), :].T)
            phi[:, span(j, PIECE)] = hi
            plo[:, span(j, PIECE)] = lo

    @pl.when(chain)
    def _():
        @pl.loop(0, 8)
        def _(j):
            rows = span(j, 128)
            hi, lo = split2(pick_rows(df, j, 128))
            dhi[rows, :] = hi
            dlo[rows, :] = lo
            hi, lo = split2(pick_rows(pf, j, 128))
            oh[rows, :] = hi
            oh[pl.ds(pl.multiple_of(BS + j * 128, 128), 128), :] = lo

        @pl.loop(0, 4)
        def _(j):
            rows = span(j, PIECE)
            th = dhi[rows, :]
            ph = oh[:BS, :]
            m = nn(th, ph) + nn(dlo[rows, :], ph) + nn(th, oh[BS:, :])
            hi, lo = split2(m.T)
            mhi[:, rows] = hi
            mlo[:, rows] = lo

    late_turn = jnp.logical_and(chain, k <= 2)

    @pl.when(jnp.logical_not(late_turn))
    def _():
        turn_panel()

    for q in range(16):
        ohr[q // 2, :, q % 2 * 128:(q % 2 + 1) * 128] = one_hot(idx_ref[q:q + 1, :], c * PIECE)

    def half(p, h):
        hi, lo = split2(xbuf[span(p, PD), :])
        three = jnp.concatenate(split3(serp[span(p, PD), :]), axis=0)

        @pl.when(core == 1)
        def _():
            hand_copy(p, h).wait_recv()

        for q in range(4):
            d = 4 * h + q
            cols = span(d, PIECE)
            a = times(hi, lo, phi[:, cols], plo[:, cols])
            b = nn(three, ohr[d])
            v = b[:PD] + (b[PD:2 * PD] + b[2 * PD:]) - a

            @pl.when(core == 0)
            def _():
                zbuf[p, h, q] = v

            @pl.when(core == 1)
            def _():
                total = v + zin[p, h, q]

                @pl.when(d == c)
                def _():
                    rbuf[chip, p] = total

                @pl.when(d != c)
                def _():
                    zbuf[p, h, q] = total
                    z_copy(p, h, q).start()

        @pl.when(core == 0)
        def _():
            hand_copy(p, h).start()

    def arrive(i):
        x_copy(0, i, zp).wait_recv()

    def forward(i, first=0, last=4):
        for e, (cond, row) in list(enumerate(edges))[first:last]:
            @pl.when(cond)
            def _():
                x_copy(e, i, row).start()

    solves = jnp.logical_and(chain, final)
    early = jnp.logical_and(r == 15, c == 6)

    @pl.when(via_dev)
    def _():
        @pl.loop(0, CHUNKS)
        def _(i):
            sum_copy(0, i).wait_recv()
            hop_copy(i).start()

    @pl.when(bulk)
    def _():
        @pl.loop(0, CHUNKS)
        def _(i):
            arrive(i)

            forward(i, 0, 2)

            @pl.when(jnp.logical_not(solves))
            def _():
                forward(i, 2, 4)

            @pl.when(chain)
            def _():
                hi, lo = split2(xbuf[span(i, CD), :])
                obuf[i] = times(hi, lo, mhi[...], mlo[...])

                @pl.when(core == 1)
                def _():
                    pair_copy(i).wait_recv()
                    obuf[i] = obuf[i] + pin[i]

                @pl.when(takes)
                def _():
                    sum_copy(chip - 1, i).wait_recv()
                    obuf[i] = obuf[i] + abuf[chip - 1, i]

                @pl.when(final)
                def _():
                    for s in range(CHIPS - 1):
                        @pl.when(jnp.logical_or(s == chip - 1, jnp.logical_and(s == 0, chip == 3)))
                        def _():
                            sum_copy(s, i).wait_recv()
                            obuf[i] = obuf[i] + abuf[s, i]
                    sum_copy(3, i).wait_recv()
                    obuf[i] = abuf[3, i] - obuf[i]

                send_out(i)

            @pl.when(solves)
            def _():
                forward(i, 2, 4)

            @pl.when(jnp.logical_and(early, i >= 2))
            def _():
                half(i // 2 - 1, i % 2)

        @pl.when(late_turn)
        def _():
            turn_panel()

        @pl.loop(jnp.where(early, CHUNKS - 2, 0), CHUNKS)
        def _(i):
            half(i // 2, i % 2)

    @pl.when(jnp.logical_not(bulk))
    def _():
        @pl.loop(0, CHUNKS + 2)
        def _(i):
            @pl.when(i < CHUNKS)
            def _():
                arrive(i)
                forward(i)

            @pl.when(i >= 2)
            def _():
                half(i // 2 - 1, i % 2)

    def put_solved(v):
        t = v.T
        sol_ref[...] = jnp.where(jnp.full((64, DATES), core, jnp.int32) == 1, t[64:, :DATES], t[:64, :DATES])

    @pl.when(sol_src)
    def _():
        for d in range(COLS):
            @pl.when(d != c)
            def _():
                s_copy(d).start()
        lane = pl.multiple_of((r % 2) * 512 + chip * 128, 128)
        put_solved(xbuf[:, pl.ds(lane, 128)])

    @pl.when(jnp.logical_not(sol_src))
    def _():
        s_copy(c).wait_recv()
        put_solved(sbuf[...])

    @pl.loop(0, CHIPS)
    def _(s):
        @pl.when(jnp.logical_not(jnp.logical_and(core == 1, s == chip)))
        def _():
            @pl.loop(0, PAIRS)
            def _(p):
                z_wait(s, p)

    total = (rbuf[0] + rbuf[1]) + (rbuf[2] + rbuf[3])
    res_ref[...] = total.reshape(ALL, PIECE)[:DATES, :]

    @pl.loop(0, CHUNKS)
    def _(i):
        @pl.when(jnp.logical_and(gives, chain))
        def _():
            g_copy(c, i).wait_send()

        for e, (cond, row) in enumerate(edges):
            @pl.when(cond)
            def _():
                x_copy(e, i, row).wait_send()

        @pl.when(uses_d)
        def _():
            pair_copy(i).wait_send()

        @pl.when(jnp.logical_or(via_src, via_dev))
        def _():
            via_copy(i).wait_send()

        @pl.when(core == 0)
        def _():
            hand_copy(i // 2, i % 2).wait_send()

        @pl.when(core == 1)
        def _():
            for q in range(4):
                @pl.when(4 * (i % 2) + q != c)
                def _():
                    z_copy(i // 2, i % 2, q).wait_send()

    @pl.when(sol_src)
    def _():
        for d in range(COLS):
            @pl.when(d != c)
            def _():
                s_copy(d).wait_send()


def body(series, point_order, step_block, panel, diag_inverse):
    idx = point_order.reshape(16, 128)
    vmem = pl.BlockSpec(memory_space=pltpu.VMEM)
    hbm = pl.BlockSpec(memory_space=pl.ANY)
    dma = pltpu.SemaphoreType.DMA
    residual, solved = pl.pallas_call(
        kernel,
        out_shape=(
            jax.ShapeDtypeStruct((DATES, PIECE), F32),
            jax.ShapeDtypeStruct((64, DATES), F32),
        ),
        in_specs=[pl.BlockSpec(memory_space=pltpu.SMEM), vmem, vmem, hbm, hbm],
        out_specs=(vmem, vmem),
        scratch_shapes=[
            pltpu.VMEM((2 * BS, BS), F32),
            pltpu.VMEM((2 * BS, BS), F32),
            pltpu.VMEM((BS, 2 * BS), BF16),
            pltpu.VMEM((BS, 2 * BS), BF16),
            pltpu.VMEM((BS, BS), BF16),
            pltpu.VMEM((BS, BS), BF16),
            pltpu.VMEM((BS, BS), BF16),
            pltpu.VMEM((BS, BS), BF16),
            pltpu.VMEM((2 * BS, BS), BF16),
            pltpu.VMEM((COLS, PIECE, PIECE), BF16),
            pltpu.VMEM((ALL, PIECE), F32),
            pltpu.VMEM((7, ALL, PIECE), F32),
            pltpu.VMEM((ALL, BS), F32),
            pltpu.VMEM((CHUNKS, CD, BS), F32),
            pltpu.VMEM((CHIPS, CHUNKS, CD, BS), F32),
            pltpu.VMEM((CHUNKS, CD, BS), F32),
            pltpu.VMEM((PAIRS, 2, 4, PD, PIECE), F32),
            pltpu.VMEM((PAIRS, 2, 4, PD, PIECE), F32),
            pltpu.VMEM((CHIPS, PAIRS, PD, PIECE), F32),
            pltpu.VMEM((ALL, 128), F32),
            dma((8,)),
            dma((8,)),
            dma((CHUNKS,)),
            dma((7, CHUNKS)),
            dma((4, CHUNKS)),
            dma((CHUNKS,)),
            dma((CHUNKS,)),
            dma((CHUNKS,)),
            dma((CHUNKS,)),
            dma((CHIPS, CHUNKS)),
            dma((PAIRS, 2, 4)),
            dma((CHIPS, PAIRS)),
            dma((PAIRS, 2)),
            dma((PAIRS, 2)),
            dma((COLS,)),
            dma,
        ],
        compiler_params=pltpu.CompilerParams(
            collective_id=0, has_side_effects=True, vmem_limit_bytes=60 * 1024 * 1024
        ),
    )(step_block, idx, series, panel, diag_inverse)
    return solved, residual.T


def solution(mesh):
    in_specs = (P(None, ("rows", "cols")), P("rows"), P(), P("rows", "cols"), P("rows", None))
    out_specs = (P(("rows", "cols"), None), P(("rows", "cols"), None))
    return jax.shard_map(body, mesh=mesh, in_specs=in_specs, out_specs=out_specs, check_vma=False)
```
